128 devices in a mesh: gx: 8 (over x, y_lo), gy: 16 (over y_hi, z, core).
Axes of the slice: x: 4, y: 4 (y_hi: 2, y_lo: 2; y = y_hi * 2 + y_lo), z: 4, core: 2. Of those that a mesh axis runs over, the one named last changes fastest.
Arguments:
- coarse_velocity: float32 [3, 32, 256, 128], P(None, 'gx', 'gy'), may hold values from -6 to 6
- coarse_stress: float32 [6, 32, 256, 128], P(None, 'gx', 'gy'), may hold values from -6 to 6
- coarse_material: float32 [3, 32, 256, 128], P(None, 'gx', 'gy'), may hold values from 0.5 to 2
- fine_velocity: float32 [3, 96, 384, 256], P(None, 'gx', 'gy'), may hold values from -6 to 6
- fine_stress: float32 [6, 96, 384, 256], P(None, 'gx', 'gy'), may hold values from -6 to 6
- fine_material: float32 [3, 96, 384, 256], P(None, 'gx', 'gy'), may hold values from 0.5 to 2
- fault_slip: float32 [96, 384], P('gx', 'gy'), may hold values from 0 to 0.5
- initial_shear: float32 [96, 384], P('gx', 'gy'), may hold values from -6 to 6
- normal_stress: float32 [96, 384], P('gx', 'gy'), may hold values from 0.5 to 2.5
- fault_mask: int32 [96, 384], P('gx', 'gy'), may hold values 0 or 1
- zone_ids: int32 [96, 384], P('gx', 'gy'), may hold values from 0 to 3
- static_friction: float32 [4], replicated, may hold values from 0.5 to 0.8
- friction_drop: float32 [4], replicated, may hold values from 0.1 to 0.4
- weakening_distance: float32 [4], replicated, may hold values from 0.05 to 0.5
- owner_rows: int32 [2, 32, 128], P(None, 'gx'), may hold values from 85 to 171, as said below
Outputs:
- coarse_velocity_next: float32 [3, 32, 256, 128], P(None, 'gx', 'gy')
- coarse_stress_next: float32 [6, 32, 256, 128], P(None, 'gx', 'gy')
- fine_velocity_next: float32 [3, 96, 384, 256], P(None, 'gx', 'gy')
- fine_stress_next: float32 [6, 96, 384, 256], P(None, 'gx', 'gy')
- fault_slip_next: float32 [96, 384], P('gx', 'gy')
The draws below stay inside these ranges and needn't reach their ends.
Inputs may be any that keep to these rules, and one draw needn't show every extreme that they name: owner_rows[0] lies within one row of 86 and owner_rows[1] within one row of 170; both ends of both ranges are taken.
All inputs are finite; a program needn't handle non-finite values. No bound on the sum of `fault_mask` on one device may be relied on, other than what follows from the above.
Results may differ from the reference program's by a relative error of at most 0.00002.
Values sent between devices are 32-bit elements; how exact they have to be, the bound alone decides.
No kernel may reach another device: no remote copies, remote signals or barrier semaphores. Data moves between devices by JAX's collectives and lax.ppermute only.
A program may use at most 128 MiB of HBM per device.

```python
import math
import jax
import jax.numpy as jnp
from jax import lax

FY = 256
ZONES = 4
NXC = 32
NYC = 256
NZC = 128
NXF = 96
NZF = 384


def draw_owner_rows(key, part):
    key = jax.random.fold_in(key, 11)
    first_key, second_key = jax.random.split(key)
    lower_jitter = jax.random.randint(first_key, (NXC, NZC), -1, 2)
    upper_jitter = jax.random.randint(second_key, (NXC, NZC), -1, 2)
    lower_jitter = lower_jitter.at[0, 0].set(-1).at[NXC - 1, NZC - 1].set(1)
    upper_jitter = upper_jitter.at[0, 0].set(1).at[NXC - 1, NZC - 1].set(-1)
    lower = NYC // 2 - FY // 6 + lower_jitter
    upper = NYC // 2 + FY // 6 + upper_jitter
    return jnp.stack([lower, upper]).astype(jnp.int32)


def set_ends(array, stream_key, low, top_value):
    spot = [jax.random.randint(jax.random.fold_in(stream_key, axis), (), 0, length) for axis, length in enumerate(array.shape)]
    widest = array.shape.index(max(array.shape))
    next_to = spot[:widest] + [(spot[widest] + 1) % array.shape[widest]] + spot[widest + 1:]
    return array.at[tuple(spot)].set(low).at[tuple(next_to)].set(top_value)


def shard_levels(stream_key, dims, cuts, smallest, largest):
    def one(dim, parts):
        draws = jax.random.uniform(jax.random.fold_in(jax.random.fold_in(stream_key, 6), dim), (parts,), jnp.float32, smallest / len(cuts), largest / len(cuts))
        return jnp.repeat(jnp.exp(draws), dims[dim] // parts).reshape((-1,) + (1,) * (len(dims) - dim - 1))

    loudness = one(*cuts[0])
    for cut in cuts[1:]:
        loudness = loudness * one(*cut)
    return loudness


def noise(stream_key, dims, spread, most, shards=(), kind=jnp.bfloat16):
    level = shard_levels(stream_key, dims, shards, -0.22, 0.18) if shards else 1.0
    values = jax.random.normal(stream_key, dims, jnp.float32) * spread * level
    return jnp.minimum(jnp.maximum(values, -most), most).astype(kind)


def setup_inputs(seed: int = 0) -> dict:
    seeds = jax.random.split(jax.random.key(seed), 16)
    coarse_velocity = noise(seeds[0], (3, NXC, NYC, NZC), 1.0, 6.0, ((1, 8), (2, 16)), jnp.float32)
    coarse_stress = noise(seeds[1], (6, NXC, NYC, NZC), 1.0, 6.0, ((1, 8), (2, 16)), jnp.float32)
    coarse_material = jnp.clip(jnp.exp(math.log(2.0) - 1.3862944 * jax.random.uniform(seeds[2], (3, NXC, NYC, NZC), jnp.float32) ** shard_levels(seeds[2], (3, NXC, NYC, NZC), ((1, 8), (2, 16)), -0.2, 0.2)), 0.5, 2.0)
    fine_velocity = noise(seeds[3], (3, NXF, NZF, FY), 1.0, 6.0, ((1, 8), (2, 16)), jnp.float32)
    fine_stress = noise(seeds[4], (6, NXF, NZF, FY), 1.0, 6.0, ((1, 8), (2, 16)), jnp.float32)
    fine_material = jnp.clip(jnp.exp(math.log(2.0) - 1.3862944 * jax.random.uniform(seeds[5], (3, NXF, NZF, FY), jnp.float32) ** shard_levels(seeds[5], (3, NXF, NZF, FY), ((1, 8), (2, 16)), -0.2, 0.2)), 0.5, 2.0)
    fault_slip = jnp.clip(0.5 * jax.random.uniform(seeds[6], (NXF, NZF), jnp.float32) ** shard_levels(seeds[6], (NXF, NZF), ((0, 8), (1, 16)), -0.2, 0.2), 0.0, 0.5)
    initial_shear = noise(seeds[7], (NXF, NZF), 1.5, 6.0, ((0, 8), (1, 16)), jnp.float32)
    normal_stress = jnp.clip(jnp.exp(math.log(2.5) - 1.609438 * jax.random.uniform(seeds[8], (NXF, NZF), jnp.float32) ** shard_levels(seeds[8], (NXF, NZF), ((0, 8), (1, 16)), -0.2, 0.2)), 0.5, 2.5)
    fault_mask = set_ends((jax.random.randint(seeds[9], (NXF, NZF), 0, 4) < 3).astype(jnp.int32), jax.random.fold_in(seeds[9], 1), 0, 1)
    zone_ids = set_ends(jax.random.randint(seeds[10], (NXF, NZF), 0, ZONES), jax.random.fold_in(seeds[10], 1), 0, ZONES - 1).astype(jnp.int32)
    static_friction = jnp.clip(jax.random.uniform(seeds[11], (ZONES,), jnp.float32, 0.5, 0.8), 0.5, 0.8)
    friction_drop = jnp.clip(jax.random.uniform(seeds[12], (ZONES,), jnp.float32, 0.1, 0.4), 0.1, 0.4)
    weakening_distance = jnp.clip(jnp.exp(jax.random.uniform(seeds[13], (ZONES,), jnp.float32, math.log(0.05), math.log(0.5))), 0.05, 0.5)
    owner_rows = draw_owner_rows(jax.random.fold_in(seeds[15], 71), 0)
    return {"coarse_velocity": coarse_velocity, "coarse_stress": coarse_stress, "coarse_material": coarse_material, "fine_velocity": fine_velocity, "fine_stress": fine_stress, "fine_material": fine_material, "fault_slip": fault_slip, "initial_shear": initial_shear, "normal_stress": normal_stress, "fault_mask": fault_mask, "zone_ids": zone_ids, "static_friction": static_friction, "friction_drop": friction_drop, "weakening_distance": weakening_distance, "owner_rows": owner_rows}


STEP_RATIO = 0.15


def shifted(values, along, forward):
    length = values.shape[along]
    edge = jnp.zeros_like(lax.slice_in_dim(values, 0, 1, axis=along))
    if forward:
        return jnp.concatenate([lax.slice_in_dim(values, 1, length, axis=along), edge], axis=along)
    return jnp.concatenate([edge, lax.slice_in_dim(values, 0, length - 1, axis=along)], axis=along)


def back_diff(values, along):
    return values - shifted(values, along, False)


def fore_diff(values, along):
    return shifted(values, along, True) - values


def trimmed(stacked, margin):
    if margin == 0:
        return stacked
    return stacked[:, margin:-margin, margin:-margin]


def velocity_step(velocity, source, material, directions, margin):
    along_x, along_y, along_z = directions
    force_x = back_diff(source[0], along_x) + back_diff(source[3], along_y) + back_diff(source[4], along_z)
    force_y = back_diff(source[3], along_x) + back_diff(source[1], along_y) + back_diff(source[5], along_z)
    force_z = back_diff(source[4], along_x) + back_diff(source[5], along_y) + back_diff(source[2], along_z)
    forces = trimmed(jnp.stack([force_x, force_y, force_z]), margin)
    return velocity + STEP_RATIO * material[0] * forces


def stress_step(stress, source, material, directions, margin):
    along_x, along_y, along_z = directions
    strain = jnp.stack([
        fore_diff(source[0], along_x),
        fore_diff(source[1], along_y),
        fore_diff(source[2], along_z),
        fore_diff(source[0], along_y) + fore_diff(source[1], along_x),
        fore_diff(source[0], along_z) + fore_diff(source[2], along_x),
        fore_diff(source[1], along_z) + fore_diff(source[2], along_y)])
    strain = trimmed(strain, margin)
    dilation = strain[0] + strain[1] + strain[2]
    lame_first = material[1]
    shear_modulus = material[2]
    update = jnp.stack([
        lame_first * dilation + 2.0 * shear_modulus * strain[0],
        lame_first * dilation + 2.0 * shear_modulus * strain[1],
        lame_first * dilation + 2.0 * shear_modulus * strain[2],
        shear_modulus * strain[3],
        shear_modulus * strain[4],
        shear_modulus * strain[5]])
    return stress + STEP_RATIO * update


def friction_step(stress, slip_state, settings):
    active, shear_start, normal_load, static_part, drop_part, inverse_distance = settings
    centre = stress.shape[3] // 2
    shear_plane = stress[3, :, :, centre]
    traction = shear_plane + shear_start
    weakened = jnp.minimum(slip_state * inverse_distance, 1.0)
    strength = normal_load * (static_part - drop_part * weakened)
    resisted = jnp.clip(traction, -strength, strength)
    slip_state = slip_state + active * STEP_RATIO * jnp.abs(traction - resisted)
    stress = stress.at[3, :, :, centre].set(shear_plane + active * (resisted - traction))
    return stress, slip_state


def with_bounds(velocity, bounds):
    velocity = velocity.at[:, :, :, 0].set(bounds[0])
    return velocity.at[:, :, :, -1].set(bounds[1])


def fault_settings(fault_mask, initial_shear, normal_stress, zone_ids, static_friction, friction_drop, weakening_distance):
    zone_count = static_friction.shape[0]
    onehot = (zone_ids[:, :, None] == jnp.arange(zone_count, dtype=jnp.int32)[None, None, :]).astype(jnp.float32)
    static_part = jnp.sum(onehot * static_friction, axis=2)
    drop_part = jnp.sum(onehot * friction_drop, axis=2)
    inverse_distance = jnp.sum(onehot * (1.0 / weakening_distance), axis=2)
    return (fault_mask.astype(jnp.float32), initial_shear, normal_stress, static_part, drop_part, inverse_distance)


def block_mean(velocity, start):
    face_cells = lax.slice_in_dim(velocity, start, start + 3, axis=3)
    grouped = face_cells.reshape(face_cells.shape[0], face_cells.shape[1] // 3, 3, face_cells.shape[2] // 3, 3, 3)
    return jnp.mean(grouped, axis=(2, 4, 5))


def restrict(velocity):
    across = velocity.shape[3]
    return jnp.stack([block_mean(velocity, 0), block_mean(velocity, across - 3)])


def inserted(velocity, selectors, restricted):
    for face in range(2):
        velocity = velocity * (1.0 - selectors[face]) + selectors[face] * restricted[face][:, :, None, :]
    return velocity


def reference(coarse_velocity, coarse_stress, coarse_material, fine_velocity, fine_stress, fine_material, fault_slip, initial_shear, normal_stress, fault_mask, zone_ids, static_friction, friction_drop, weakening_distance, owner_rows):
    row_ids = jnp.arange(NYC, dtype=jnp.int32)
    selectors = (row_ids[None, None, :, None] == owner_rows[:, :, None, :]).astype(jnp.float32)
    coupling_plane = jnp.sum(selectors[:, None] * coarse_velocity[None], axis=3)
    bounds = jnp.repeat(jnp.repeat(coupling_plane, 3, axis=2), 3, axis=3)
    settings = fault_settings(fault_mask, initial_shear, normal_stress, zone_ids, static_friction, friction_drop, weakening_distance)
    velocity = fine_velocity
    stress = fine_stress
    slip_state = fault_slip
    for substep in range(3):
        velocity = with_bounds(velocity_step(velocity, stress, fine_material, (0, 2, 1), 0), bounds)
        stress = stress_step(stress, velocity, fine_material, (0, 2, 1), 0)
        stress, slip_state = friction_step(stress, slip_state, settings)
    restricted = restrict(velocity)
    coarse_next = velocity_step(coarse_velocity, coarse_stress, coarse_material, (0, 1, 2), 0)
    coarse_next = inserted(coarse_next, selectors, restricted)
    coarse_stress_next = stress_step(coarse_stress, coarse_next, coarse_material, (0, 1, 2), 0)
    return (coarse_next, coarse_stress_next, velocity, stress, slip_state)
```

```python
import jax
import jax.numpy as jnp
from jax import lax
from jax.experimental import pallas as pl
from jax.experimental.pallas import tpu as pltpu
from jax.sharding import PartitionSpec as P

STEP_RATIO = 0.15
F32 = jnp.float32
FINE_S = (0, 2, 1, 4, 3, 5)
FINE_V = (0, 2, 1)
COARSE_S = (0, 1, 2, 3, 4, 5)
COARSE_V = (0, 1, 2)
VMEM = pl.BlockSpec(memory_space=pltpu.VMEM)
SMEM = pl.BlockSpec(memory_space=pltpu.SMEM)
PARAMS = pltpu.CompilerParams(vmem_limit_bytes=32 * 1024 * 1024)


def call(kernel, outs, specs, *args):
    return pl.pallas_call(
        kernel,
        out_shape=tuple(jax.ShapeDtypeStruct(shape, F32) for shape in outs),
        in_specs=list(specs),
        out_specs=tuple(VMEM for _ in outs),
        compiler_params=PARAMS,
    )(*args)


def ring(value, axis, steps):
    count = lax.axis_size(axis)
    return lax.ppermute(value, axis, [(i, (i + steps) % count) for i in range(count)])


def iota(shape, along):
    return lax.broadcasted_iota(jnp.int32, shape, along)


def behind(a, along, edge):
    return jnp.where(iota(a.shape, along) == 0, edge, pltpu.roll(a, 1, along))


def ahead(a, along, edge):
    last = a.shape[along] - 1
    return jnp.where(iota(a.shape, along) == last, edge, pltpu.roll(a, last, along))


def velocity_plane(v, s, s_prev, rows, buoyancy):
    xx, bb, ll, xb, xl, bl = s
    p_xx, p_xb, p_xl = s_prev
    r_xb, r_bb, r_bl = rows
    f_x = (xx - p_xx) + (xb - behind(xb, 0, r_xb)) + (xl - behind(xl, 1, 0.0))
    f_b = (xb - p_xb) + (bb - behind(bb, 0, r_bb)) + (bl - behind(bl, 1, 0.0))
    f_l = (xl - p_xl) + (bl - behind(bl, 0, r_bl)) + (ll - behind(ll, 1, 0.0))
    scale = STEP_RATIO * buoyancy
    return (v[0] + scale * f_x, v[1] + scale * f_b, v[2] + scale * f_l)


def stress_plane(s, v, v_next, rows, lame, shear):
    vx, vb, vl = v
    nx, nb, nl = v_next
    rx, rb, rl = rows
    e_x = nx - vx
    e_b = ahead(vb, 0, rb) - vb
    e_l = ahead(vl, 1, 0.0) - vl
    e_xb = (ahead(vx, 0, rx) - vx) + (nb - vb)
    e_xl = (ahead(vx, 1, 0.0) - vx) + (nl - vl)
    e_bl = (ahead(vl, 0, rl) - vl) + (ahead(vb, 1, 0.0) - vb)
    common = (STEP_RATIO * lame) * (e_x + e_b + e_l)
    one = STEP_RATIO * shear
    two = 2.0 * one
    return (
        s[0] + (common + two * e_x),
        s[1] + (common + two * e_b),
        s[2] + (common + two * e_l),
        s[3] + one * e_xb,
        s[4] + one * e_xl,
        s[5] + one * e_bl,
    )


def own_cells(place, depth):
    shape = (depth, 128)
    return iota(shape, 1) == place[1] * (depth // 3) + iota(shape, 0) // 3


def pack_kernel(fs, cs, cv, rows_ref, place, xsend, zsend, coupling):
    nx, nz, _ = fs.shape[1:]
    cx, cy, cz = cs.shape[1:]
    for k, c in enumerate((0, 4, 3)):
        xsend[k * nz : (k + 1) * nz, :] = fs[c, nx - 1]
    for k, c in enumerate((0, 3, 4)):
        at = 3 * nz + k * 8
        xsend[at : at + 8, 0:128] = cs[c, cx - 1, 0:8]
        xsend[at : at + 8, 128:256] = cs[c, cx - 1, 8:16]
    zsend[...] = jnp.zeros_like(zsend)
    for k, c in enumerate((4, 2, 5)):
        for x in range(nx):
            zsend[k * nx + x, :] = fs[c, x, nz - 1]
    for k, c in enumerate((3, 1, 5)):
        for x in range(cx):
            zsend[40 + k * cx + x, 0:128] = cs[c, x, cy - 1]
    for f in range(2):
        for x in range(cx):
            here = place[1] * cy + iota((cy, cz), 0) == rows_ref[f, x : x + 1, :]
            for c in range(3):
                row = jnp.sum(jnp.where(here, cv[c, x], 0.0), axis=0, keepdims=True)
                coupling[(f * 3 + c) * cx + x : (f * 3 + c) * cx + x + 1, :] = row


def fault_kernel(slip, shear, normal, mask, zone, static, drop, distance, out, buf):
    nx, nz = slip.shape
    buf[...] = jnp.zeros_like(buf)
    for k, ref in enumerate((slip, shear, normal, mask, zone)):
        buf[16 * k : 16 * k + nx, 0:nz] = ref[...].astype(F32)
    turned = buf[...].T[0:nz]
    parts = [turned] + [pltpu.roll(turned, 128 - 16 * k, 1) for k in range(1, 5)]
    zero = jnp.zeros_like(turned)
    static_part, drop_part, inverse = zero, zero, zero
    for k in range(4):
        hit = parts[4] == float(k)
        static_part = jnp.where(hit, static[k], static_part)
        drop_part = jnp.where(hit, drop[k], drop_part)
        inverse = jnp.where(hit, 1.0 / jnp.full_like(zero, distance[k]), inverse)
    for k, part in enumerate((parts[0], parts[1], parts[2], parts[3], static_part, drop_part, inverse)):
        out[k] = part


def fine_velocity_kernel(last, with_coarse, *refs):
    if with_coarse:
        v, s, m, xr, zr, bounds, place, cxs, czs, out, xsend, zsend = refs
    elif last:
        v, s, m, xr, zr, bounds, place, out, xsend, zsend, share = refs
    else:
        v, s, m, xr, zr, bounds, place, out, xsend, zsend = refs
    nx, nz, ny = v.shape[1:]
    lane = iota((nz, ny), 1)
    cells = own_cells(place, nz)
    has_x = place[0] > 0
    has_z = place[1] > 0

    def column(f, c, x):
        at = (f * 3 + c) * (nx // 3) + x
        return jnp.sum(jnp.where(cells, bounds[at : at + 1, :], 0.0), axis=1, keepdims=True)

    columns = [[[column(f, c, x) for x in range(nx // 3)] for c in range(3)] for f in range(2)]
    zsend[...] = jnp.zeros_like(zsend)
    sums = {}
    for x in range(nx):
        here = [s[c, x] for c in FINE_S]
        if x == 0:
            before = [jnp.where(has_x, xr[k * nz : (k + 1) * nz, :], 0.0) for k in range(3)]
        else:
            before = [s[c, x - 1] for c in (0, 4, 3)]
        rows = [jnp.where(has_z, zr[k * nx + x : k * nx + x + 1, :], 0.0) for k in range(3)]
        new = velocity_plane([v[c, x] for c in FINE_V], here, before, rows, m[0, x])
        for k, c in enumerate(FINE_V):
            val = jnp.where(lane == 0, columns[0][c][x // 3], new[k])
            val = jnp.where(lane == ny - 1, columns[1][c][x // 3], val)
            out[c, x] = val
            if x == 0:
                xsend[k * nz : (k + 1) * nz, :] = val
            zsend[k * nx + x : k * nx + x + 1, :] = val[0:1]
            if last:
                sums[c, x // 3] = val if x % 3 == 0 else sums[c, x // 3] + val
    if with_coarse:
        xsend[3 * nz :, :] = cxs[...]
        zsend[40:, :] = czs[...]
    if last:
        for f in range(2):
            face = lane < 3 if f == 0 else lane >= ny - 3
            for c in range(3):
                for x in range(nx // 3):
                    at = (f * 3 + c) * (nx // 3) + x
                    total = jnp.sum(jnp.where(face, sums[c, x], 0.0), axis=1, keepdims=True)
                    row = jnp.sum(jnp.where(cells, total, 0.0), axis=0, keepdims=True)
                    share[at : at + 1, :] = row * (1.0 / 27.0)


def fine_stress_kernel(last, s, v, m, xr, zr, settings, slip, place, out, slip_out, *sends):
    nx, nz, ny = s.shape[1:]
    has_x = place[0] < place[2] - 1
    has_z = place[1] < place[3] - 1
    for x in range(nx):
        here = [v[c, x] for c in FINE_V]
        if x == nx - 1:
            after = [jnp.where(has_x, xr[k * nz : (k + 1) * nz, :], 0.0) for k in range(3)]
        else:
            after = [v[c, x + 1] for c in FINE_V]
        rows = [jnp.where(has_z, zr[k * nx + x : k * nx + x + 1, :], 0.0) for k in range(3)]
        new = stress_plane([s[c, x] for c in FINE_S], here, after, rows, m[1, x], m[2, x])
        for k, c in enumerate(FINE_S):
            out[c, x] = new[k]
    lane = iota((nz, 128), 1)
    half = ny // 2
    planes = [out[3, x, :, half:] for x in range(nx)]
    shear_plane = jnp.zeros((nz, 128), F32)
    for x in range(nx):
        moved = planes[x] if x == 0 else pltpu.roll(planes[x], x, 1)
        shear_plane = jnp.where(lane == x, moved, shear_plane)
    old = slip[...]
    traction = shear_plane + settings[1]
    weakened = jnp.minimum(old * settings[6], 1.0)
    strength = settings[2] * (settings[4] - settings[5] * weakened)
    resisted = jnp.clip(traction, -strength, strength)
    active = settings[3]
    fresh = old + active * STEP_RATIO * jnp.abs(traction - resisted)
    fixed = shear_plane + active * (resisted - traction)
    for x in range(nx):
        moved = fixed if x == 0 else pltpu.roll(fixed, 128 - x, 1)
        out[3, x, :, half:] = jnp.where(lane == 0, moved, planes[x])
    if last:
        turned = jnp.concatenate([fresh, jnp.zeros((128 - nz, 128), F32)], axis=0).T
        slip_out[...] = turned[0:nx, 0:nz]
        return
    slip_out[...] = fresh
    xsend, zsend = sends
    for k, c in enumerate((0, 4, 3)):
        xsend[k * nz : (k + 1) * nz, :] = out[c, nx - 1]
    zsend[...] = jnp.zeros_like(zsend)
    for k, c in enumerate((4, 2, 5)):
        for x in range(nx):
            zsend[k * nx + x : k * nx + x + 1, :] = out[c, x, nz - 1 : nz]


def coarse_velocity_kernel(cv, cs, cm, xr, zr, rows_ref, place, out, xsend, zsend):
    nx, ny, nz = cv.shape[1:]
    nzf = xr.shape[0] - 24
    has_x = place[0] > 0
    has_y = place[1] > 0
    xsend[...] = jnp.zeros_like(xsend)
    zsend[...] = jnp.zeros_like(zsend)
    for x in range(nx):
        here = [cs[c, x] for c in COARSE_S]
        if x == 0:
            before = []
            for k in range(3):
                at = nzf + 8 * k
                plane = jnp.concatenate([xr[at : at + 8, 0:128], xr[at : at + 8, 128:256]], axis=0)
                before.append(jnp.where(has_x, plane, 0.0))
        else:
            before = [cs[c, x - 1] for c in (0, 3, 4)]
        rows = [jnp.where(has_y, zr[40 + k * nx + x : 41 + k * nx + x, 0:128], 0.0) for k in range(3)]
        new = velocity_plane([cv[c, x] for c in COARSE_V], here, before, rows, cm[0, x])
        for c in range(3):
            out[c, x] = new[c]
            zsend[c * nx + x : c * nx + x + 1, 0:128] = new[c][0:1]
            if x == 0:
                xsend[8 * c : 8 * c + 8, 0:128] = new[c][0:8]
                xsend[8 * c : 8 * c + 8, 128:256] = new[c][8:16]
    for f in range(2):
        xsend[24 + f : 25 + f, 0:128] = rows_ref[f, 0:1, :].astype(F32)


def coarse_stress_kernel(cv, cs, cm, xr, zr, rows_ref, rest, rest_next, place, v_out, s_out):
    nx, ny, nz = cv.shape[1:]
    base = xr.shape[0] - 32
    has_x = place[0] < place[2] - 1
    has_y = place[1] < place[3] - 1
    row_ids = place[1] * ny + iota((ny, nz), 0)

    def inserted(plane, c, x):
        for f in range(2):
            if x < nx:
                hit = row_ids == rows_ref[f, x : x + 1, :]
                at = (f * 3 + c) * nx + x
                value = rest[at : at + 1, :]
            else:
                hit = row_ids.astype(F32) == xr[base + 24 + f : base + 25 + f, 0:128]
                value = rest_next[f * 3 + c : f * 3 + c + 1, :]
            plane = jnp.where(hit, value, plane)
        return plane

    planes = [[inserted(cv[c, x], c, x) for c in range(3)] for x in range(nx)]
    edge = []
    for c in range(3):
        at = base + 8 * c
        plane = jnp.concatenate([xr[at : at + 8, 0:128], xr[at : at + 8, 128:256]], axis=0)
        edge.append(jnp.where(has_x, inserted(plane, c, nx), 0.0))
    planes.append(edge)
    for x in range(nx):
        for c in range(3):
            v_out[c, x] = planes[x][c]
        rows = [jnp.where(has_y, zr[40 + k * nx + x : 41 + k * nx + x, 0:128], 0.0) for k in range(3)]
        new = stress_plane([cs[c, x] for c in COARSE_S], planes[x], planes[x + 1], rows, cm[1, x], cm[2, x])
        for c in range(6):
            s_out[c, x] = new[c]


def spread(value):
    total = value + ring(value, "gy", 4) + ring(value, "gy", 8) + ring(value, "gy", 12)
    return total + ring(total, "gy", 1) + ring(total, "gy", 2) + ring(total, "gy", 3)


def body(
    coarse_velocity,
    coarse_stress,
    coarse_material,
    fine_velocity,
    fine_stress,
    fine_material,
    fault_slip,
    initial_shear,
    normal_stress,
    fault_mask,
    zone_ids,
    static_friction,
    friction_drop,
    weakening_distance,
    owner_rows,
):
    nx, nz, ny = fine_velocity.shape[1:]
    cx = coarse_velocity.shape[1]
    place = jnp.stack(
        [lax.axis_index("gx"), lax.axis_index("gy"), lax.axis_size("gx"), lax.axis_size("gy")]
    ).astype(jnp.int32)
    shares = (6 * cx, 128)
    xsize = 3 * nz
    xsend, zsend, coupling = call(
        pack_kernel,
        [(xsize + 24, 256), (56, 256), shares],
        [VMEM] * 4 + [SMEM],
        fine_stress, coarse_stress, coarse_velocity, owner_rows, place,
    )
    bounds = spread(coupling)
    xr, zr = ring(xsend, "gx", 1), ring(zsend, "gy", 1)
    settings = pl.pallas_call(
        fault_kernel,
        out_shape=jax.ShapeDtypeStruct((7, nz, 128), F32),
        in_specs=[VMEM] * 5 + [SMEM] * 3,
        out_specs=VMEM,
        scratch_shapes=[pltpu.VMEM((128, 128), F32)],
        compiler_params=PARAMS,
    )(fault_slip, initial_shear, normal_stress, fault_mask, zone_ids, static_friction, friction_drop, weakening_distance)
    slip = settings[0]
    coarse_moved, cxs, czs = call(
        coarse_velocity_kernel,
        [coarse_velocity.shape, (32, 256), (16, 256)],
        [VMEM] * 6 + [SMEM],
        coarse_velocity, coarse_stress, coarse_material, xr, zr, owner_rows, place,
    )
    velocity, stress = fine_velocity, fine_stress
    for step in range(3):
        last, coarse_too = step == 2, step == 1
        args = [velocity, stress, fine_material, xr, zr, bounds, place]
        outs = [velocity.shape, (xsize + 32 * coarse_too, 256), (40 + 16 * coarse_too, 256)]
        specs = [VMEM] * 6 + [SMEM]
        if coarse_too:
            args += [cxs, czs]
            specs += [VMEM] * 2
        if last:
            outs.append(shares)
        velocity, xsend, zsend, *more = call(
            lambda *refs, last=last, coarse_too=coarse_too: fine_velocity_kernel(last, coarse_too, *refs),
            outs, specs, *args,
        )
        if last:
            restricted = spread(more[0])
            first = jnp.concatenate([restricted[cx * k : cx * k + 1] for k in range(6)], axis=0)
            restricted_next = ring(first, "gx", -1)
        xr, zr = ring(xsend, "gx", -1), ring(zsend, "gy", -1)
        if coarse_too:
            coarse_xr, coarse_zr = xr, zr
        outs = [stress.shape]
        outs += [fault_slip.shape] if last else [(nz, 128), (xsize, 256), (40, 256)]
        stress, slip, *sends = call(
            lambda *refs, last=last: fine_stress_kernel(last, *refs),
            outs, [VMEM] * 7 + [SMEM],
            stress, velocity, fine_material, xr, zr, settings, slip, place,
        )
        if not last:
            xr, zr = ring(sends[0], "gx", 1), ring(sends[1], "gy", 1)
    coarse_next, coarse_stress_next = call(
        coarse_stress_kernel,
        [coarse_velocity.shape, coarse_stress.shape],
        [VMEM] * 8 + [SMEM],
        coarse_moved, coarse_stress, coarse_material, coarse_xr, coarse_zr, owner_rows, restricted, restricted_next, place,
    )
    return (coarse_next, coarse_stress_next, velocity, stress, slip)


def solution(mesh):
    grid = P(None, "gx", "gy", None)
    plane = P("gx", "gy")
    return jax.shard_map(
        body,
        mesh=mesh,
        in_specs=(grid,) * 6 + (plane,) * 5 + (P(),) * 3 + (P(None, "gx", None),),
        out_specs=(grid,) * 4 + (plane,),
        check_vma=False,
    )
```

```python
import jax
import jax.numpy as jnp
from jax import lax
from jax.experimental import pallas as pl
from jax.experimental.pallas import tpu as pltpu
from jax.sharding import PartitionSpec as P

STEP_RATIO = 0.15
F32 = jnp.float32
FINE_S = (0, 2, 1, 4, 3, 5)
FINE_V = (0, 2, 1)
COARSE_S = (0, 1, 2, 3, 4, 5)
COARSE_V = (0, 1, 2)
VMEM = pl.BlockSpec(memory_space=pltpu.VMEM)
SMEM = pl.BlockSpec(memory_space=pltpu.SMEM)
HBM = pl.BlockSpec(memory_space=pltpu.HBM)
PARAMS = pltpu.CompilerParams(vmem_limit_bytes=32 * 1024 * 1024)


def call(kernel, outs, specs, *args):
    return pl.pallas_call(
        kernel,
        out_shape=tuple(jax.ShapeDtypeStruct(shape, F32) for shape in outs),
        in_specs=list(specs),
        out_specs=tuple(VMEM for _ in outs),
        compiler_params=PARAMS,
    )(*args)


def ring(value, axis, steps):
    count = lax.axis_size(axis)
    return lax.ppermute(value, axis, [(i, (i + steps) % count) for i in range(count)])


def iota(shape, along):
    return lax.broadcasted_iota(jnp.int32, shape, along)


def b_behind(a, edge):
    return jnp.where(iota(a.shape, 0) == 0, edge, pltpu.roll(a, 1, 0))


def b_ahead(a, edge):
    last = a.shape[0] - 1
    return jnp.where(iota(a.shape, 0) == last, edge, pltpu.roll(a, last, 0))


def l_behind(a):
    return jnp.where(iota(a.shape, 1) == 0, 0.0, pltpu.roll(a, 1, 1))


def l_ahead(a):
    last = a.shape[1] - 1
    return jnp.where(iota(a.shape, 1) == last, 0.0, pltpu.roll(a, last, 1))


def velocity_plane(v, s, s_prev, rows, buoyancy, b_back=b_behind, l_back=l_behind):
    xx, bb, ll, xb, xl, bl = s
    p_xx, p_xb, p_xl = s_prev
    r_xb, r_bb, r_bl = rows
    f_x = (xx - p_xx) + (xb - b_back(xb, r_xb)) + (xl - l_back(xl))
    f_b = (xb - p_xb) + (bb - b_back(bb, r_bb)) + (bl - l_back(bl))
    f_l = (xl - p_xl) + (bl - b_back(bl, r_bl)) + (ll - l_back(ll))
    scale = STEP_RATIO * buoyancy
    return (v[0] + scale * f_x, v[1] + scale * f_b, v[2] + scale * f_l)


def stress_plane(s, v, v_next, rows, lame, shear, b_fore=b_ahead, l_fore=l_ahead):
    vx, vb, vl = v
    nx, nb, nl = v_next
    rx, rb, rl = rows
    e_x = nx - vx
    e_b = b_fore(vb, rb) - vb
    e_l = l_fore(vl) - vl
    e_xb = (b_fore(vx, rx) - vx) + (nb - vb)
    e_xl = (l_fore(vx) - vx) + (nl - vl)
    e_bl = (b_fore(vl, rl) - vl) + (l_fore(vb) - vb)
    common = (STEP_RATIO * lame) * (e_x + e_b + e_l)
    one = STEP_RATIO * shear
    two = 2.0 * one
    return (
        s[0] + (common + two * e_x),
        s[1] + (common + two * e_b),
        s[2] + (common + two * e_l),
        s[3] + one * e_xb,
        s[4] + one * e_xl,
        s[5] + one * e_bl,
    )


BEFORE_X, AFTER_X, BEFORE_Z, AFTER_Z, FIRST_CELL, FIRST_ROW = range(6)


def make_flags(cells, rows):
    gx, gy = lax.axis_index("gx"), lax.axis_index("gy")
    last_x, last_y = lax.axis_size("gx") - 1, lax.axis_size("gy") - 1
    values = (gx > 0, gx < last_x, gy > 0, gy < last_y, gy * cells, gy * rows, gx, gy)
    values = jnp.stack([jnp.asarray(v).astype(F32) for v in values])
    return jnp.broadcast_to(values[:, None], (8, 256))


def has(flags, which):
    return flags[which : which + 1, :] > 0.5


def own_cells(flags, depth):
    shape = (depth, 128)
    row = iota(shape, 0)
    cell = iota(shape, 1) - jnp.where(row < 27, row // 3, -1)
    return cell.astype(F32) == flags[FIRST_CELL : FIRST_CELL + 1, 0:128]


def own_rows(flags, shape):
    return iota(shape, 0).astype(F32) + flags[FIRST_ROW : FIRST_ROW + 1, 0:128]


RIM = 8


def part_of(field, refs):
    if field < 3:
        return refs[0], field
    if field < 9:
        return refs[1], field - 3
    return refs[2], field - 9


def pack_kernel(
    fv, fs, fm, cs, cv, cm, slip, shear, normal, mask, zone, rows_hbm, flags,
    up, down, coupling, raw,
    top_v, top_s, top_m, low_v, low_s, low_m, cz_buf, cv_buf, cs_low, cm_low, rows_ref, slip_buf, shear_buf, normal_buf, mask_buf, zone_buf, turn, sem,
):
    nx, nz, ny = fv.shape[1:]
    cx, cy, cz = cs.shape[1:]
    fault = (slip_buf, shear_buf, normal_buf, mask_buf, zone_buf)
    moves = [(cv, cv_buf), (rows_hbm, rows_ref)]
    moves += list(zip((slip, shear, normal, mask, zone), fault))
    for k, c in enumerate((3, 1, 5)):
        moves.append((cs.at[c, :, cy - 8 : cy, :], cz_buf.at[k]))
    moves.append((cs.at[:, :, 0:8, :], cs_low))
    moves.append((cm.at[0, :, 0:8, :], cm_low))
    early = len(moves)
    for src, top, low in ((fv, top_v, low_v), (fs, top_s, low_s), (fm, top_m, low_m)):
        moves.append((src.at[:, :, nz - 8 : nz, :], top))
        moves.append((src.at[:, :, 0:8, :], low))
    copies = [pltpu.make_async_copy(src, dst, sem.at[i]) for i, (src, dst) in enumerate(moves)]
    for copy in copies:
        copy.start()
    for copy in copies[:early]:
        copy.wait()
    for f in range(2):
        for x in range(cx):
            here = own_rows(flags, (cy, cz)) == rows_ref[f, x : x + 1, :].astype(F32)
            for c in range(3):
                row = jnp.sum(jnp.where(here, cv_buf[c, x], 0.0), axis=0, keepdims=True)
                at = (f * 3 + c) * cx + x
                coupling[at : at + 1, :] = row
    turn[...] = jnp.zeros_like(turn)
    for k, ref in enumerate(fault):
        turn[16 * k : 16 * k + nx, 0:nz] = ref[...].astype(F32)
    turned = turn[...].T[0:nz]
    raw[...] = turned
    at = nx * 32
    up[at:, :] = jnp.zeros((24, ny), F32)
    for k in range(3):
        for x in range(cx):
            up[at + k * cx + x : at + k * cx + x + 1, 0:128] = cz_buf[k, x, 7:8]
    up[at + 16 : at + 24, 0:128] = turned[nz - 8 :]
    down[nx * 40 :, :] = jnp.zeros((48, ny), F32)
    down[nx * 40 : nx * 40 + 8, 0:128] = turned[0:8]
    for c in range(10):
        for x in range(cx):
            if c < 3:
                row = cv_buf[c, x, 0:1]
            elif c < 9:
                row = cs_low[c - 3, x, 0:1]
            else:
                row = cm_low[x, 0:1]
            at = nx * 40 + 8 + c * cx + x
            down[at : at + 1, 0:128] = row
    for copy in copies[early:]:
        copy.wait()
    tops, lows = (top_v, top_s, top_m), (low_v, low_s, low_m)
    sub = iota((RIM, ny), 0)

    def rolled(tile, by):
        return pltpu.roll(tile, by % RIM, 0) if by % RIM else tile

    def step(x, _):
        def take(refs, field):
            ref, c = part_of(field, refs)
            return ref[c, x]

        for t in range(3):
            tile = rolled(take(tops, 4 * t), -6)
            for i in range(1, 4):
                tile = jnp.where(sub // 2 == i, rolled(take(tops, 4 * t + i), 2 * i - 6), tile)
            up[pl.ds(x * 32 + 8 * t, 8), :] = tile
        tile = rolled(take(tops, 3 + 2), -5)
        tile = jnp.where(sub == 1, rolled(take(tops, 3 + 4), -4), tile)
        tile = jnp.where(sub == 2, rolled(take(tops, 3 + 5), -3), tile)
        up[pl.ds(x * 32 + 24, 8), :] = tile
        for t in range(5):
            tile = jnp.where(sub < 3, take(lows, 2 * t), rolled(take(lows, 2 * t + 1), 3))
            if t < 2:
                tile = jnp.where(sub < 6, tile, rolled(take(lows, 10 + t), 6))
            down[pl.ds(x * 40 + 8 * t, 8), :] = tile
        return 0

    lax.fori_loop(0, nx, step, 0)


def rim_kernel(from_below, from_above, fs, cs, raw, parts_of, flags, left, right, rim, xsend, settings, total):
    total[...] = left[...] + right[...]
    nx, nz, ny = fs.shape[1:]
    cx = cs.shape[1]
    has_below, has_above = has(flags, BEFORE_Z), has(flags, AFTER_Z)
    sub = iota((RIM, ny), 0)

    def rolled(tile, by):
        return pltpu.roll(tile, by % RIM, 0) if by % RIM else tile

    def step(x, _):
        last = jnp.where(has_below, from_below[pl.ds(x * 32 + 24, 8), :], 0.0)
        for t in range(3):
            tile = jnp.where(has_below, from_below[pl.ds(x * 32 + 8 * t, 8), :], 0.0)
            for i in range(4):
                field = 4 * t + i
                below = rolled(tile, 6 - 2 * i)
                extra = {5: 5, 7: 4, 8: 3}.get(field)
                if extra is not None:
                    below = jnp.where(sub == 5, rolled(last, extra), below)
                t2, i2 = divmod(field, 2)
                if field < 10:
                    above = from_above[pl.ds(x * 40 + 8 * t2, 8), :]
                    above = rolled(above, -3 * i2)
                else:
                    above = rolled(from_above[pl.ds(x * 40 + 8 * (field - 10), 8), :], 2)
                above = jnp.where(has_above, above, 0.0)
                rim[field, x] = jnp.where(sub < 4, above, below)
        return 0

    lax.fori_loop(0, nx, step, 0)
    for k, c in enumerate((0, 4, 3)):
        xsend[32 * k : 32 * k + nz, :] = fs[c, nx - 1]
        xsend[32 * k + nz : 32 * k + 32, :] = rim[3 + c, nx - 1]
    for k, c in enumerate((0, 3, 4)):
        xsend[96 + 8 * k : 104 + 8 * k, 0:128] = cs[c, cx - 1, 0:8]
        xsend[96 + 8 * k : 104 + 8 * k, 128:256] = cs[c, cx - 1, 8:16]
    xsend[120:, :] = jnp.zeros((8, ny), F32)
    for k, c in enumerate((0, 3, 4)):
        at = nx * 40 + 8 + (3 + c) * cx + cx - 1
        xsend[120 + k : 121 + k, 0:128] = jnp.where(has_above[:, 0:128], from_above[at : at + 1, 0:128], 0.0)
    below = jnp.where(has_below[:, 0:128], from_below[nx * 32 + 16 :, 0:128], 0.0)
    above = jnp.where(has_above[:, 0:128], from_above[nx * 40 : nx * 40 + 8, 0:128], 0.0)
    turned = jnp.concatenate([raw[...], jnp.where(iota((RIM, 128), 0) < 4, above, below)], axis=0)
    settings[0] = turned
    for k in (1, 2, 3):
        settings[k] = pltpu.roll(turned, 128 - 16 * k, 1)
    zones = pltpu.roll(turned, 128 - 64, 1)
    for k in range(3):
        value = jnp.zeros_like(turned)
        for zone in range(4):
            value = jnp.where(zones == float(zone), parts_of[4 * k + zone : 4 * k + zone + 1, :], value)
        settings[4 + k] = value


def ring_back(a, _):
    return pltpu.roll(a, 1, 0)


def ring_fore(a, _):
    return pltpu.roll(a, a.shape[0] - 1, 0)


def reader(ref, rim, first):
    if ref.shape[2] == 32:
        return lambda c, x: ref[c, x]
    return lambda c, x: jnp.concatenate([ref[c, x], rim[first + c, x]], axis=0)


def held_column(bounds, cells, face, c, x):
    at = (face * 3 + c) * (bounds.shape[0] // 6) + x
    return jnp.sum(jnp.where(cells, bounds[at : at + 1, :], 0.0), axis=1, keepdims=True)


def held(value, columns):
    lane = iota(value.shape, 1)
    value = jnp.where(lane == 0, columns[0], value)
    return jnp.where(lane == value.shape[1] - 1, columns[1], value)


def merged(a):
    return jnp.where(iota((a.shape[0], 128), 1) < 64, a[:, 0:128], a[:, a.shape[1] - 128 :])


def fine_velocity_kernel(step, v_ref, s_ref, m_ref, rim, xr, bounds_a, bounds_b, flags, *refs):
    refs = list(refs)
    if step == 1:
        cxs = refs.pop(0)
    if step == 2:
        left, right = refs.pop(0), refs.pop(0)
        refs.pop()[...] = left[...] + right[...]
    out, xsend = refs
    bounds = bounds_a[...] + bounds_b[...]
    v, s, m = reader(v_ref, rim, 0), reader(s_ref, rim, 3), reader(m_ref, rim, 9)
    nx, nz, ny = v_ref.shape[1], 32, v_ref.shape[3]
    cells = own_cells(flags, nz)
    has_x = has(flags, BEFORE_X)
    for x in range(nx):
        here = [s(c, x) for c in FINE_S]
        if x % 3 == 0:
            columns = [[held_column(bounds, cells, f, c, x // 3) for f in range(2)] for c in range(3)]
        if x == 0:
            before = [jnp.where(has_x, xr[k * nz : (k + 1) * nz, :], 0.0) for k in range(3)]
        else:
            before = [s(c, x - 1) for c in (0, 4, 3)]
        old = [v(c, x) for c in FINE_V]
        buoyancy = m(0, x)
        new = velocity_plane(old, here, before, (0.0,) * 3, buoyancy, ring_back)
        for k, c in enumerate(FINE_V):
            val = held(new[k], columns[c])
            out[c, x] = val
            if x == 0:
                xsend[k * nz : (k + 1) * nz, :] = val
        if step == 0 and x == 0:
            xsend[3 * nz :, :] = jnp.zeros_like(xsend[3 * nz :, :])
            xsend[3 * nz :, 0:128] = merged(buoyancy)[0:16]
            xsend[3 * nz : 3 * nz + 8, 128:256] = merged(buoyancy)[16:24]
    if step == 1:
        xsend[3 * nz :, :] = cxs[...]


def share_kernel(v, s, m, xr, bounds_a, bounds_b, flags, share):
    nx, nz, ny = v.shape[1:]
    cx, own = nx // 3, nz - RIM
    bounds = bounds_a[...] + bounds_b[...]
    lane = iota((own, 128), 1)
    cells = own_cells(flags, own)

    def l_back(a):
        return pltpu.roll(a, 1, 1)

    columns = [[[held_column(bounds, cells, f, c, x) for f in range(2)] for c in range(3)] for x in range(cx)]
    sums = {}
    before = [jnp.zeros((own, 128), F32)] * 3
    for x in range(nx):
        here = [merged(s[c, x]) for c in FINE_S]
        old = [merged(v[c, x, 0:own, :]) for c in FINE_V]
        rows = [here[k][nz - 1 : nz] for k in (3, 1, 5)]
        here = [a[0:own] for a in here]
        new = velocity_plane(old, here, before, rows, merged(m[0, x]), b_behind, l_back)
        before = [here[0], here[3], here[4]]
        for k, c in enumerate(FINE_V):
            val = held(new[k], columns[x // 3][c])
            sums[c, x // 3] = val if x % 3 == 0 else sums[c, x // 3] + val
    buoyancy = jnp.concatenate([xr[96:112, 0:128], xr[96:104, 128:256]], axis=0)
    ahead = [-STEP_RATIO * buoyancy * plane for plane in before]
    for f in range(2):
        face = lane < 3 if f == 0 else lane >= 125
        free = (lane == 1) | (lane == 2) if f == 0 else (lane == 125) | (lane == 126)
        for k, c in enumerate(FINE_V):
            at = f * 3 + c
            for x in range(cx):
                total = jnp.sum(jnp.where(face, sums[c, x], 0.0), axis=1, keepdims=True)
                row = jnp.sum(jnp.where(cells, total, 0.0), axis=0, keepdims=True)
                share[at * cx + x : at * cx + x + 1, :] = row * (1.0 / 27.0)
            total = jnp.sum(jnp.where(free, ahead[k], 0.0), axis=1, keepdims=True)
            row = jnp.sum(jnp.where(cells, total, 0.0), axis=0, keepdims=True)
            share[6 * cx + at : 6 * cx + at + 1, :] = row * (1.0 / 27.0)
    share[6 * cx + 6 :, :] = jnp.zeros_like(share[6 * cx + 6 :, :])


def fine_stress_kernel(step, s_ref, v_ref, m_ref, rim, xr, settings, slip, flags, *refs):
    last = step == 2
    copies = []
    nx, nz, ny = s_ref.shape[1], 32, s_ref.shape[3]
    own = nz - RIM
    if last:
        final, v_final, slip_out, out, sem = refs
        copies.append(pltpu.make_async_copy(v_ref.at[:, :, 0:own, :], v_final, sem.at[0]))
        copies[0].start()
    else:
        out, slip_out, xsend = refs
    v, s, m = reader(v_ref, rim, 0), reader(s_ref, rim, 3), reader(m_ref, rim, 9)
    has_x = has(flags, AFTER_X)
    half = ny // 2
    lane = iota((nz, 128), 1)
    shear_plane = jnp.zeros((nz, 128), F32)
    for x in range(nx):
        here = [v(c, x) for c in FINE_V]
        if x == nx - 1:
            after = [jnp.where(has_x, xr[k * nz : (k + 1) * nz, :], 0.0) for k in range(3)]
        else:
            after = [v(c, x + 1) for c in FINE_V]
        old = [s(c, x) for c in FINE_S]
        new = stress_plane(old, here, after, (0.0,) * 3, m(1, x), m(2, x), ring_fore)
        for k, c in enumerate(FINE_S):
            out[c, x] = new[k]
            if c == 3:
                moved = new[k][:, half:]
                moved = moved if x == 0 else pltpu.roll(moved, x, 1)
                shear_plane = jnp.where(lane == x, moved, shear_plane)
        if last:
            for first, end in ((0, 3), (4, 6)):
                at = len(copies)
                copies.append(
                    pltpu.make_async_copy(
                        out.at[first:end, x, 0:own, :], final.at[first:end, x], sem.at[at]
                    )
                )
                copies[at].start()
    old = slip[...]
    traction = shear_plane + settings[1]
    weakened = jnp.minimum(old * settings[6], 1.0)
    strength = settings[2] * (settings[4] - settings[5] * weakened)
    resisted = jnp.clip(traction, -strength, strength)
    active = settings[3]
    fresh = old + active * STEP_RATIO * jnp.abs(traction - resisted)
    fixed = shear_plane + active * (resisted - traction)
    for x in range(nx):
        moved = fixed if x == 0 else pltpu.roll(fixed, 128 - x, 1)
        out[3, x, :, half : half + 128] = jnp.where(lane == 0, moved, out[3, x, :, half : half + 128])
    if last:
        copies.append(pltpu.make_async_copy(out.at[3, :, 0:own, :], final.at[3], sem.at[len(copies)]))
        copies[-1].start()
        turned = jnp.concatenate([fresh, jnp.zeros((128 - nz, 128), F32)], axis=0).T
        slip_out[...] = turned[0:nx, 0:own]
        for copy in copies:
            copy.wait()
        return
    slip_out[...] = fresh
    for k, c in enumerate((0, 4, 3)):
        xsend[k * nz : (k + 1) * nz, :] = out[c, nx - 1]


def coarse_velocity_kernel(cv, cs, cm, xr, below, above, rows_ref, flags, out, xsend, next_rows, cs_near, cm_near):
    nx, ny, nz = cv.shape[1:]
    has_x, has_y = has(flags, BEFORE_X)[:, 0:128], has(flags, BEFORE_Z)[:, 0:128]
    more = has(flags, AFTER_Z)[:, 0:128]
    low, high = below.shape[0] - 24, above.shape[0] - 40
    cs_near[...] = cs[...]
    cm_near[...] = cm[...]
    xsend[...] = jnp.zeros_like(xsend)
    next_rows[3 * nx :, :] = jnp.zeros_like(next_rows[3 * nx :, :])

    def ahead(field, x):
        at = high + field * nx + x
        return jnp.where(more, above[at : at + 1, 0:128], 0.0)

    for x in range(nx):
        here = [cs[c, x] for c in COARSE_S]
        here_row = [ahead(3 + c, x) for c in COARSE_S]
        if x == 0:
            before, before_row = [], []
            for k in range(3):
                at = 96 + 8 * k
                plane = jnp.concatenate([xr[at : at + 8, 0:128], xr[at : at + 8, 128:256]], axis=0)
                before.append(jnp.where(has_x, plane, 0.0))
                before_row.append(jnp.where(has_x, xr[120 + k : 121 + k, 0:128], 0.0))
        else:
            before = [cs[c, x - 1] for c in (0, 3, 4)]
            before_row = [ahead(3 + c, x - 1) for c in (0, 3, 4)]
        rows = [jnp.where(has_y, below[low + k * nx + x : low + k * nx + x + 1, 0:128], 0.0) for k in range(3)]
        new = velocity_plane([cv[c, x] for c in COARSE_V], here, before, rows, cm[0, x])
        last = [here[k][ny - 1 : ny] for k in (3, 1, 5)]
        old_row = [ahead(c, x) for c in COARSE_V]
        new_row = velocity_plane(old_row, here_row, before_row, last, ahead(9, x), lambda a, edge: edge)
        for c in range(3):
            out[c, x] = new[c]
            next_rows[c * nx + x : c * nx + x + 1, :] = new_row[c]
            if x == 0:
                xsend[8 * c : 8 * c + 8, 0:128] = new[c][0:8]
                xsend[8 * c : 8 * c + 8, 128:256] = new[c][8:16]
    for f in range(2):
        xsend[24 + f : 25 + f, 0:128] = rows_ref[f, 0:1, :].astype(F32)


def coarse_stress_kernel(cv, cs, cm, xr, zr, rows_ref, rest, rest_next, rest_before, flags, _, v_out, s_out):
    nx, ny, nz = cv.shape[1:]
    base = xr.shape[0] - 32
    has_x, has_y = has(flags, AFTER_X)[:, 0:128], has(flags, AFTER_Z)[:, 0:128]
    row_ids = own_rows(flags, (ny, nz))

    before_x = has(flags, BEFORE_X)[:, 0:128]

    def inserted(plane, c, x):
        for f in range(2):
            if x < nx:
                hit = row_ids == rows_ref[f, x : x + 1, :].astype(F32)
            else:
                hit = row_ids == xr[base + 24 + f : base + 25 + f, 0:128]
            at = (f * 3 + c) * nx + x % nx
            more = 6 * nx + f * 3 + c
            if x == 0:
                from_before = jnp.where(before_x, rest_before[more : more + 1, :], 0.0)
                value = rest[at : at + 1, :] + from_before
            elif x < nx:
                value = rest[at : at + 1, :]
            else:
                value = rest_next[at : at + 1, :] + rest[more : more + 1, :]
            plane = jnp.where(hit, value, plane)
        return plane

    planes = [[inserted(cv[c, x], c, x) for c in range(3)] for x in range(nx)]
    edge = []
    for c in range(3):
        at = base + 8 * c
        plane = jnp.concatenate([xr[at : at + 8, 0:128], xr[at : at + 8, 128:256]], axis=0)
        edge.append(jnp.where(has_x, inserted(plane, c, nx), 0.0))
    planes.append(edge)
    for x in range(nx):
        for c in range(3):
            v_out[c, x] = planes[x][c]
        rows = [jnp.where(has_y, zr[k * nx + x : k * nx + x + 1, :], 0.0) for k in range(3)]
        new = stress_plane([cs[c, x] for c in COARSE_S], planes[x], planes[x + 1], rows, cm[1, x], cm[2, x])
        for c in range(6):
            s_out[c, x] = new[c]


def swap(value, axis, bit):
    count = lax.axis_size(axis)
    return lax.ppermute(value, axis, [(i, i ^ bit) for i in range(count)])


def spread(value, turns):
    for bits in turns:
        value = value + swap(value, "gy", bits)
    return value


def body(
    coarse_velocity,
    coarse_stress,
    coarse_material,
    fine_velocity,
    fine_stress,
    fine_material,
    fault_slip,
    initial_shear,
    normal_stress,
    fault_mask,
    zone_ids,
    static_friction,
    friction_drop,
    weakening_distance,
    owner_rows,
):
    nx, nz, ny = fine_velocity.shape[1:]
    cx, cy, cz = coarse_velocity.shape[1:]
    flags = make_flags(nz // 3, cy)
    shares = (6 * cx, cz)
    fault = (fault_slip, initial_shear, normal_stress, fault_mask, zone_ids)
    fields = (fine_velocity, fine_stress, fine_material)
    given = [
        pltpu.with_memory_space_constraint(a, pltpu.HBM)
        for a in fields + (coarse_stress, coarse_velocity, coarse_material) + fault + (owner_rows,)
    ]
    up, down, coupling, raw = pl.pallas_call(
        pack_kernel,
        out_shape=[
            jax.ShapeDtypeStruct(shape, F32)
            for shape in ((nx * 32 + 24, ny), (nx * 40 + 48, ny), shares, (nz, 128))
        ],
        in_specs=[HBM] * len(given) + [VMEM],
        out_specs=[VMEM] * 4,
        scratch_shapes=[pltpu.VMEM((a.shape[0], nx, 8, ny), F32) for a in fields * 2]
        + [pltpu.VMEM((3, cx, 8, cz), F32), pltpu.VMEM(coarse_velocity.shape, F32)]
        + [pltpu.VMEM((6, cx, 8, cz), F32), pltpu.VMEM((cx, 8, cz), F32)]
        + [pltpu.VMEM(owner_rows.shape, jnp.int32)]
        + [pltpu.VMEM(a.shape, a.dtype) for a in fault]
        + [pltpu.VMEM((128, 128), F32), pltpu.SemaphoreType.DMA((18,))],
        compiler_params=PARAMS,
    )(*given, flags)
    from_below, from_above = ring(up, "gy", 1), ring(down, "gy", -1)
    coupling = spread(coupling, (1, 2))
    parts_of = jnp.concatenate([static_friction, friction_drop, 1.0 / weakening_distance, jnp.zeros(4, F32)])
    parts_of = jnp.broadcast_to(parts_of[:, None], (16, 128))
    rim, xsend, settings, bounds = call(
        rim_kernel,
        [(12, nx, RIM, ny), (128, ny), (7, 32, 128), shares],
        [VMEM] * 9,
        from_below, from_above, fine_stress, coarse_stress, raw, parts_of, flags, coupling, swap(coupling, "gy", 6),
    )
    slip = settings[0]
    xr = ring(xsend, "gx", 1)
    bounds = (bounds, swap(bounds, "gy", 8))
    coarse_moved, cxs, coarse_zr, coarse_stress, coarse_material = call(
        coarse_velocity_kernel,
        [coarse_velocity.shape, (32, ny), (16, cz), coarse_stress.shape, coarse_material.shape],
        [VMEM] * 8,
        coarse_velocity, coarse_stress, coarse_material, xr, from_below, from_above, owner_rows, flags,
    )
    velocity, stress = fine_velocity, fine_stress

    def velocity_half(step, xr, *more):
        outs = [(3, nx, 32, ny), (96 + (16, 32, 0)[step], ny)]
        if step == 2:
            outs.append(more[0].shape)
        return call(
            lambda *refs: fine_velocity_kernel(step, *refs),
            outs, [VMEM] * (8 + len(more)),
            velocity, stress, fine_material, rim, xr, *bounds, flags, *more,
        )

    def stress_half(step, xr):
        return call(
            lambda *refs: fine_stress_kernel(step, *refs),
            [(6, nx, 32, ny), (32, 128), (96, ny)], [VMEM] * 8,
            stress, velocity, fine_material, rim, xr, settings, slip, flags,
        )

    velocity, xsend = velocity_half(0, xr)
    next_x = ring(xsend, "gx", -1)
    stress, slip, xsend = stress_half(0, next_x)
    velocity, xsend = velocity_half(1, ring(xsend, "gx", 1), cxs)
    coarse_xr = ring(xsend, "gx", -1)
    stress, slip, xsend = stress_half(1, coarse_xr)
    (share,) = call(share_kernel, [(32, cz)], [VMEM] * 7, velocity, stress, fine_material, next_x, *bounds, flags)
    share, xsend = lax.optimization_barrier((share, xsend))
    share = spread(share, (1,))
    velocity, xsend, share = velocity_half(2, ring(xsend, "gx", 1), share, swap(share, "gy", 2))
    restricted = spread(share, (6, 8))
    restricted_next, restricted_before = ring(restricted, "gx", -1), ring(restricted, "gx", 1)
    xr = ring(xsend, "gx", -1)
    stress, velocity, slip = pl.pallas_call(
        lambda *refs: fine_stress_kernel(2, *refs),
        out_shape=[jax.ShapeDtypeStruct(a.shape, F32) for a in (fine_stress, fine_velocity, fault_slip)],
        in_specs=[VMEM] * 8,
        out_specs=[pl.BlockSpec(memory_space=pl.ANY)] * 2 + [VMEM],
        scratch_shapes=[pltpu.VMEM((6, nx, 32, ny), F32), pltpu.SemaphoreType.DMA((2 * nx + 2,))],
        compiler_params=PARAMS,
    )(stress, velocity, fine_material, rim, xr, settings, slip, flags)
    coarse_next, coarse_stress_next = call(
        coarse_stress_kernel,
        [coarse_velocity.shape, coarse_stress.shape],
        [VMEM] * 11,
        coarse_moved, coarse_stress, coarse_material, coarse_xr, coarse_zr, owner_rows, restricted, restricted_next,
        restricted_before, flags, slip,
    )
    return (coarse_next, coarse_stress_next, velocity, stress, slip)


def solution(mesh):
    grid = P(None, "gx", "gy", None)
    plane = P("gx", "gy")
    return jax.shard_map(
        body,
        mesh=mesh,
        in_specs=(grid,) * 6 + (plane,) * 5 + (P(),) * 3 + (P(None, "gx", None),),
        out_specs=(grid,) * 4 + (plane,),
        check_vma=False,
    )
```

```python
import jax
import jax.numpy as jnp
from jax import lax
from jax.experimental import pallas as pl
from jax.experimental.pallas import tpu as pltpu
from jax.sharding import PartitionSpec as P

STEP_RATIO = 0.15
F32 = jnp.float32
FINE_S = (0, 2, 1, 4, 3, 5)
FINE_V = (0, 2, 1)
COARSE_S = (0, 1, 2, 3, 4, 5)
COARSE_V = (0, 1, 2)
VMEM = pl.BlockSpec(memory_space=pltpu.VMEM)
SMEM = pl.BlockSpec(memory_space=pltpu.SMEM)
HBM = pl.BlockSpec(memory_space=pltpu.HBM)
PARAMS = pltpu.CompilerParams(vmem_limit_bytes=8 * 1024 * 1024)


def call(kernel, outs, specs, *args):
    return pl.pallas_call(
        kernel,
        out_shape=tuple(jax.ShapeDtypeStruct(shape, F32) for shape in outs),
        in_specs=list(specs),
        out_specs=tuple(VMEM for _ in outs),
        compiler_params=PARAMS,
    )(*args)


def ring(value, axis, steps):
    count = lax.axis_size(axis)
    return lax.ppermute(value, axis, [(i, (i + steps) % count) for i in range(count)])


def iota(shape, along):
    return lax.broadcasted_iota(jnp.int32, shape, along)


def b_behind(a, edge):
    return jnp.where(iota(a.shape, 0) == 0, edge, pltpu.roll(a, 1, 0))


def b_ahead(a, edge):
    last = a.shape[0] - 1
    return jnp.where(iota(a.shape, 0) == last, edge, pltpu.roll(a, last, 0))


def l_behind(a):
    return jnp.where(iota(a.shape, 1) == 0, 0.0, pltpu.roll(a, 1, 1))


def l_ahead(a):
    last = a.shape[1] - 1
    return jnp.where(iota(a.shape, 1) == last, 0.0, pltpu.roll(a, last, 1))


def velocity_plane(v, s, s_prev, rows, buoyancy, b_back=b_behind, l_back=l_behind):
    xx, bb, ll, xb, xl, bl = s
    p_xx, p_xb, p_xl = s_prev
    r_xb, r_bb, r_bl = rows
    f_x = (xx - p_xx) + (xb - b_back(xb, r_xb)) + (xl - l_back(xl))
    f_b = (xb - p_xb) + (bb - b_back(bb, r_bb)) + (bl - l_back(bl))
    f_l = (xl - p_xl) + (bl - b_back(bl, r_bl)) + (ll - l_back(ll))
    scale = STEP_RATIO * buoyancy
    return (v[0] + scale * f_x, v[1] + scale * f_b, v[2] + scale * f_l)


def stress_plane(s, v, v_next, rows, lame, shear, b_fore=b_ahead, l_fore=l_ahead):
    vx, vb, vl = v
    nx, nb, nl = v_next
    rx, rb, rl = rows
    e_x = nx - vx
    e_b = b_fore(vb, rb) - vb
    e_l = l_fore(vl) - vl
    e_xb = (b_fore(vx, rx) - vx) + (nb - vb)
    e_xl = (l_fore(vx) - vx) + (nl - vl)
    e_bl = (b_fore(vl, rl) - vl) + (l_fore(vb) - vb)
    common = (STEP_RATIO * lame) * (e_x + e_b + e_l)
    one = STEP_RATIO * shear
    two = 2.0 * one
    return (
        s[0] + (common + two * e_x),
        s[1] + (common + two * e_b),
        s[2] + (common + two * e_l),
        s[3] + one * e_xb,
        s[4] + one * e_xl,
        s[5] + one * e_bl,
    )


BEFORE_X, AFTER_X, BEFORE_Z, AFTER_Z, FIRST_CELL, FIRST_ROW = range(6)


def make_flags(cells, rows):
    gx, gy = lax.axis_index("gx"), lax.axis_index("gy")
    last_x, last_y = lax.axis_size("gx") - 1, lax.axis_size("gy") - 1
    values = (gx > 0, gx < last_x, gy > 0, gy < last_y, gy * cells, gy * rows, gx, gy)
    values = jnp.stack([jnp.asarray(v).astype(F32) for v in values])
    return jnp.broadcast_to(values[:, None], (8, 256))


def has(flags, which):
    return flags[which : which + 1, :] > 0.5


def own_cells(flags, depth):
    shape = (depth, 128)
    row = iota(shape, 0)
    cell = iota(shape, 1) - jnp.where(row < 27, row // 3, -1)
    return cell.astype(F32) == flags[FIRST_CELL : FIRST_CELL + 1, 0:128]


def own_rows(flags, shape):
    return iota(shape, 0).astype(F32) + flags[FIRST_ROW : FIRST_ROW + 1, 0:128]


RIM = 8


def part_of(field, refs):
    if field < 3:
        return refs[0], field
    if field < 9:
        return refs[1], field - 3
    return refs[2], field - 9


def coupling_kernel(cv, rows_hbm, flags, _, coupling, cv_buf, rows_ref, sem):
    cx, cy, cz = cv.shape[1:]
    moves = ((cv, cv_buf), (rows_hbm, rows_ref))
    copies = [pltpu.make_async_copy(src, dst, sem.at[i]) for i, (src, dst) in enumerate(moves)]
    for copy in copies:
        copy.start()
    for copy in copies:
        copy.wait()
    ids = own_rows(flags, (cy, cz))
    for f in range(2):
        for x in range(cx):
            here = ids == rows_ref[f, x : x + 1, :].astype(F32)
            for c in range(3):
                row = jnp.sum(jnp.where(here, cv_buf[c, x], 0.0), axis=0, keepdims=True)
                at = (f * 3 + c) * cx + x
                coupling[at : at + 1, :] = row


def pack_kernel(
    fv, fs, fm, cs, cv, cm, slip, shear, normal, mask, zone, static, drop, distance, _,
    up, down, raw,
    top_v, top_s, top_m, low_v, low_s, low_m, cz_buf, cv_low, cs_low, cm_low, static_buf, drop_buf, distance_buf, slip_buf, shear_buf, normal_buf, mask_buf, zone_buf, turn, sem,
):
    nx, nz, ny = fv.shape[1:]
    cx, cy, cz = cs.shape[1:]
    fault = (slip_buf, shear_buf, normal_buf, mask_buf, zone_buf)
    zoned = (static_buf, drop_buf, distance_buf)
    moves = list(zip((slip, shear, normal, mask, zone, static, drop, distance), fault + zoned))
    moves.append((cv.at[:, :, 0:8, :], cv_low))
    for k, c in enumerate((3, 1, 5)):
        moves.append((cs.at[c, :, cy - 8 : cy, :], cz_buf.at[k]))
    moves.append((cs.at[:, :, 0:8, :], cs_low))
    moves.append((cm.at[0, :, 0:8, :], cm_low))
    early = len(moves)
    for src, top, low in ((fv, top_v, low_v), (fs, top_s, low_s), (fm, top_m, low_m)):
        moves.append((src.at[:, :, nz - 8 : nz, :], top))
        moves.append((src.at[:, :, 0:8, :], low))
    copies = [pltpu.make_async_copy(src, dst, sem.at[i]) for i, (src, dst) in enumerate(moves)]
    for copy in copies:
        copy.start()
    for copy in copies[:early]:
        copy.wait()
    turn[...] = jnp.zeros_like(turn)
    for k, ref in enumerate(fault):
        turn[16 * k : 16 * k + nx, 0:nz] = ref[...].astype(F32)
    turned = turn[...].T[0:nz]
    zones = pltpu.roll(turned, 128 - 64, 1)
    group = iota(turned.shape, 1) // 16
    for k in range(3):
        value = jnp.zeros_like(turned)
        for zone_id in range(4):
            part = zoned[k][zone_id]
            if k == 2:
                part = 1.0 / jnp.full(turned.shape, part)
            value = jnp.where(zones == float(zone_id), part, value)
        turned = jnp.where(group == 5 + k, pltpu.roll(value, 16 * (5 + k), 1), turned)
    raw[...] = turned
    at = nx * 32
    up[at:, :] = jnp.zeros((24, ny), F32)
    for k in range(3):
        for x in range(cx):
            up[at + k * cx + x : at + k * cx + x + 1, 0:128] = cz_buf[k, x, 7:8]
    up[at + 16 : at + 24, 0:128] = turned[nz - 8 :]
    down[nx * 40 :, :] = jnp.zeros((48, ny), F32)
    down[nx * 40 : nx * 40 + 8, 0:128] = turned[0:8]
    for c in range(10):
        for x in range(cx):
            if c < 3:
                row = cv_low[c, x, 0:1]
            elif c < 9:
                row = cs_low[c - 3, x, 0:1]
            else:
                row = cm_low[x, 0:1]
            at = nx * 40 + 8 + c * cx + x
            down[at : at + 1, 0:128] = row
    for copy in copies[early:]:
        copy.wait()
    tops, lows = (top_v, top_s, top_m), (low_v, low_s, low_m)
    sub = iota((RIM, ny), 0)

    def rolled(tile, by):
        return pltpu.roll(tile, by % RIM, 0) if by % RIM else tile

    def step(x, _):
        def take(refs, field):
            ref, c = part_of(field, refs)
            return ref[c, x]

        for t in range(3):
            tile = rolled(take(tops, 4 * t), -6)
            for i in range(1, 4):
                tile = jnp.where(sub // 2 == i, rolled(take(tops, 4 * t + i), 2 * i - 6), tile)
            up[pl.ds(x * 32 + 8 * t, 8), :] = tile
        tile = rolled(take(tops, 3 + 2), -5)
        tile = jnp.where(sub == 1, rolled(take(tops, 3 + 4), -4), tile)
        tile = jnp.where(sub == 2, rolled(take(tops, 3 + 5), -3), tile)
        up[pl.ds(x * 32 + 24, 8), :] = tile
        for t in range(5):
            tile = jnp.where(sub < 3, take(lows, 2 * t), rolled(take(lows, 2 * t + 1), 3))
            if t < 2:
                tile = jnp.where(sub < 6, tile, rolled(take(lows, 10 + t), 6))
            down[pl.ds(x * 40 + 8 * t, 8), :] = tile
        return 0

    lax.fori_loop(0, nx, step, 0)


def add_up(parts):
    total = parts[0][...]
    for part in parts[1:]:
        total = total + part[...]
    return total


def fault_settings(turned):
    return [turned] + [pltpu.roll(turned, 128 - 16 * k, 1) for k in (1, 2, 3, 5, 6, 7)]


def rim_kernel(from_below, from_above, fs, fm, cs, raw, flags, rim, xsend, settings):
    nx, nz, ny = fs.shape[1:]
    cx = cs.shape[1]
    has_below, has_above = has(flags, BEFORE_Z), has(flags, AFTER_Z)
    sub = iota((RIM, ny), 0)

    def rolled(tile, by):
        return pltpu.roll(tile, by % RIM, 0) if by % RIM else tile

    def step(x, _):
        last = jnp.where(has_below, from_below[pl.ds(x * 32 + 24, 8), :], 0.0)
        for t in range(3):
            tile = jnp.where(has_below, from_below[pl.ds(x * 32 + 8 * t, 8), :], 0.0)
            for i in range(4):
                field = 4 * t + i
                below = rolled(tile, 6 - 2 * i)
                extra = {5: 5, 7: 4, 8: 3}.get(field)
                if extra is not None:
                    below = jnp.where(sub == 5, rolled(last, extra), below)
                t2, i2 = divmod(field, 2)
                if field < 10:
                    above = from_above[pl.ds(x * 40 + 8 * t2, 8), :]
                    above = rolled(above, -3 * i2)
                else:
                    above = rolled(from_above[pl.ds(x * 40 + 8 * (field - 10), 8), :], 2)
                above = jnp.where(has_above, above, 0.0)
                rim[field, x] = jnp.where(sub < 4, above, below)
        return 0

    lax.fori_loop(0, nx, step, 0)
    for k, c in enumerate((0, 4, 3)):
        xsend[32 * k : 32 * k + nz, :] = fs[c, nx - 1]
        xsend[32 * k + nz : 32 * k + 32, :] = rim[3 + c, nx - 1]
    for k, c in enumerate((0, 3, 4)):
        xsend[96 + 8 * k : 104 + 8 * k, 0:128] = cs[c, cx - 1, 0:8]
        xsend[96 + 8 * k : 104 + 8 * k, 128:256] = cs[c, cx - 1, 8:16]
    xsend[120:128, :] = jnp.zeros((8, ny), F32)
    for k, c in enumerate((0, 3, 4)):
        at = nx * 40 + 8 + (3 + c) * cx + cx - 1
        xsend[120 + k : 121 + k, 0:128] = jnp.where(has_above[:, 0:128], from_above[at : at + 1, 0:128], 0.0)
    below = jnp.where(has_below[:, 0:128], from_below[nx * 32 + 16 :, 0:128], 0.0)
    above = jnp.where(has_above[:, 0:128], from_above[nx * 40 : nx * 40 + 8, 0:128], 0.0)
    turned = jnp.concatenate([raw[...], jnp.where(iota((RIM, 128), 0) < 4, above, below)], axis=0)
    for k in (1, 2):
        at = 96 + 32 * k
        xsend[at : at + nz, :] = fm[k, nx - 1]
        xsend[at + nz : at + 32, :] = rim[9 + k, nx - 1]
    xsend[192:208, 0:128] = turned[0:16]
    xsend[192:208, 128:256] = turned[16:32]
    for k, part in enumerate(fault_settings(turned)):
        settings[k] = part


def ring_back(a, _):
    return pltpu.roll(a, 1, 0)


def ring_fore(a, _):
    return pltpu.roll(a, a.shape[0] - 1, 0)


def reader(ref, rim, first):
    if ref.shape[2] == 32:
        return lambda c, x: ref[c, x]
    return lambda c, x: jnp.concatenate([ref[c, x], rim[first + c, x]], axis=0)


def held_column(bounds, cells, face, c, x):
    at = (face * 3 + c) * (bounds.shape[0] // 6) + x
    return jnp.sum(jnp.where(cells, bounds[at : at + 1, :], 0.0), axis=1, keepdims=True)


def held(value, columns):
    lane = iota(value.shape, 1)
    value = jnp.where(lane == 0, columns[0], value)
    return jnp.where(lane == value.shape[1] - 1, columns[1], value)


def merged(a):
    return jnp.where(iota((a.shape[0], 128), 1) < 64, a[:, 0:128], a[:, a.shape[1] - 128 :])


def velocity_planes(planes, v_ref, s_ref, m_ref, rim, behind, bounds_a, bounds_b, flags, put):
    bounds = bounds_a[...] + bounds_b[...]
    v, s, m = reader(v_ref, rim, 0), reader(s_ref, rim, 3), reader(m_ref, rim, 9)
    nz = 32
    cells = own_cells(flags, nz)
    has_x = has(flags, BEFORE_X)
    columns = {}
    for x in planes:
        here = [s(c, x) for c in FINE_S]
        if x // 3 not in columns:
            columns[x // 3] = [[held_column(bounds, cells, f, c, x // 3) for f in range(2)] for c in range(3)]
        if x == 0:
            before = [jnp.where(has_x, behind[k * nz : (k + 1) * nz, :], 0.0) for k in range(3)]
        else:
            before = [s(c, x - 1) for c in (0, 4, 3)]
        old = [v(c, x) for c in FINE_V]
        new = velocity_plane(old, here, before, (0.0,) * 3, m(0, x), ring_back)
        put(x, [held(new[k], columns[x // 3][c]) for k, c in enumerate(FINE_V)])


def velocity_edge_kernel(step, v, s, m, rim, behind, bounds_a, bounds_b, flags, *refs):
    refs = list(refs)
    more = [refs.pop(0)] if step == 1 else []
    nz = 32 if step < 2 else 24

    def put(x, new):
        for k in range(3):
            refs[0 if x == 0 else 1][k * nz : (k + 1) * nz, :] = new[k][0:nz]

    planes = [0] if step == 2 else [0, v.shape[1] - 1]
    velocity_planes(planes, v, s, m, rim, behind, bounds_a, bounds_b, flags, put)
    if step == 1:
        refs[0][3 * nz :, :] = more[0][...]


def fine_velocity_kernel(v, s, m, rim, behind, bounds_a, bounds_b, flags, out):
    def put(x, new):
        for k, c in enumerate(FINE_V):
            out[c, x] = new[k]

    velocity_planes(range(v.shape[1]), v, s, m, rim, behind, bounds_a, bounds_b, flags, put)


def share_kernel(v, s, m, behind, bounds_a, bounds_b, flags, share):
    nx, nz, ny = v.shape[1:]
    cx, own = nx // 3, nz - RIM
    bounds = bounds_a[...] + bounds_b[...]
    lane = iota((own, 128), 1)
    cells = own_cells(flags, own)

    def l_back(a):
        return pltpu.roll(a, 1, 1)

    columns = [[[held_column(bounds, cells, f, c, x) for f in range(2)] for c in range(3)] for x in range(cx)]
    sums = {}
    before = [merged(behind[k * nz : k * nz + own, :]) for k in range(3)]
    for x in range(nx):
        here = [merged(s[c, x]) for c in FINE_S]
        old = [merged(v[c, x, 0:own, :]) for c in FINE_V]
        rows = [here[k][nz - 1 : nz] for k in (3, 1, 5)]
        here = [a[0:own] for a in here]
        new = velocity_plane(old, here, before, rows, merged(m[0, x]), b_behind, l_back)
        before = [here[0], here[3], here[4]]
        for k, c in enumerate(FINE_V):
            val = held(new[k], columns[x // 3][c])
            sums[c, x // 3] = val if x % 3 == 0 else sums[c, x // 3] + val
    for f in range(2):
        face = lane < 3 if f == 0 else lane >= 125
        for c in range(3):
            for x in range(cx):
                at = (f * 3 + c) * cx + x
                total = jnp.sum(jnp.where(face, sums[c, x], 0.0), axis=1, keepdims=True)
                row = jnp.sum(jnp.where(cells, total, 0.0), axis=0, keepdims=True)
                share[at : at + 1, :] = row * (1.0 / 27.0)


def stress_planes(planes, s_ref, v_ref, m_ref, rim, xr, flags, put):
    v, s, m = reader(v_ref, rim, 0), reader(s_ref, rim, 3), reader(m_ref, rim, 9)
    nx, nz, half = s_ref.shape[1], 32, s_ref.shape[3] // 2
    has_x = has(flags, AFTER_X)
    lane = iota((nz, 128), 1)
    shear_plane = jnp.zeros((nz, 128), F32)
    for x in planes:
        here = [v(c, x) for c in FINE_V]
        if x == nx - 1:
            rows = nz if xr.shape[0] >= 3 * nz else nz - RIM
            after = [jnp.where(has_x, xr[k * rows : (k + 1) * rows, :], 0.0) for k in range(3)]
            if rows < nz:
                rest = jnp.zeros((nz - rows, xr.shape[1]), F32)
                after = [jnp.concatenate([plane, rest], axis=0) for plane in after]
        else:
            after = [v(c, x + 1) for c in FINE_V]
        old = [s(c, x) for c in FINE_S]
        new = stress_plane(old, here, after, (0.0,) * 3, m(1, x), m(2, x), ring_fore)
        put(x, new)
        moved = new[4][:, half : half + 128]
        moved = moved if x == 0 else pltpu.roll(moved, x, 1)
        shear_plane = jnp.where(lane == x, moved, shear_plane)
    return shear_plane


def friction(shear_plane, settings, old):
    traction = shear_plane + settings[1]
    weakened = jnp.minimum(old * settings[6], 1.0)
    strength = settings[2] * (settings[4] - settings[5] * weakened)
    resisted = jnp.clip(traction, -strength, strength)
    active = settings[3]
    fresh = old + active * STEP_RATIO * jnp.abs(traction - resisted)
    return fresh, shear_plane + active * (resisted - traction)


def with_fault(upper, fixed, x):
    moved = fixed if x == 0 else pltpu.roll(fixed, 128 - x, 1)
    return jnp.where(iota(upper.shape, 1) == 0, moved, upper)


def stress_behind(old, v_behind, v_first, given, slip, flags, out, slip_out):
    nz, half = 32, v_behind.shape[1] // 2
    has_x = has(flags, BEFORE_X)
    here = [v_behind[k * nz : (k + 1) * nz, :] for k in range(3)]
    xx, xb, xl = (old[k * nz : (k + 1) * nz, :] for k in range(3))
    lame, shear = given[128:160, :], given[160:192, :]
    new = stress_plane((xx, xx, xx, xb, xl, xl), here, v_first, (0.0,) * 3, lame, shear, ring_fore)
    turned = jnp.concatenate([given[192:208, 0:128], given[192:208, 128:256]], axis=0)
    settings = fault_settings(turned)
    last = 11
    xl = new[4]
    before = settings[0] if slip is None else slip[...]
    fresh, fixed = friction(pltpu.roll(xl[:, half : half + 128], last, 1), settings, before)
    if slip_out is not None:
        slip_out[...] = fresh
    xl = jnp.concatenate([xl[:, 0:half], with_fault(xl[:, half:], fixed, last)], axis=1)
    for k, value in enumerate((new[0], new[3], xl)):
        out[k * nz : (k + 1) * nz, :] = jnp.where(has_x, value, 0.0)


def fine_stress_kernel(step, s, v, m, rim, xr, settings, slip, flags, *refs):
    last = step == 2
    copies = []
    nx, nz, half = s.shape[1], 32, s.shape[3] // 2
    own = nz - RIM
    if last:
        final, v_final, slip_out, mark, out, sem = refs
        mark[...] = jnp.zeros_like(mark)
        copies.append(pltpu.make_async_copy(v.at[:, :, 0:own, :], v_final, sem.at[0]))
        copies[0].start()
    else:
        if step == 0:
            v_behind, given, out, slip_out, behind, slip_behind = refs
            old, slip_before = given, None
        else:
            v_behind, given, old, slip_before, out, slip_out, behind = refs
            slip_behind = None
        stress_behind(
            old, v_behind, [v[c, 0] for c in FINE_V], given, slip_before, flags, behind, slip_behind
        )

    def put(x, new):
        for k, c in enumerate(FINE_S):
            out[c, x] = new[k]
        if last:
            for first, end in ((0, 3), (4, 6)):
                at = len(copies)
                copies.append(
                    pltpu.make_async_copy(out.at[first:end, x, 0:own, :], final.at[first:end, x], sem.at[at])
                )
                copies[at].start()

    shear_plane = stress_planes(range(nx), s, v, m, rim, xr, flags, put)
    fresh, fixed = friction(shear_plane, settings, slip[...])
    for x in range(nx):
        out[3, x, :, half:] = with_fault(out[3, x, :, half:], fixed, x)
    if last:
        copies.append(pltpu.make_async_copy(out.at[3, :, 0:own, :], final.at[3], sem.at[len(copies)]))
        copies[-1].start()
        turned = jnp.concatenate([fresh, jnp.zeros((128 - nz, 128), F32)], axis=0).T
        slip_out[...] = turned[0:nx, 0:own]
        for copy in copies:
            copy.wait()
    else:
        slip_out[...] = fresh


def coarse_velocity_kernel(cv, cs, cm, xr, below, above, rows_ref, flags, out, xsend, next_rows, cs_near, cm_near):
    nx, ny, nz = cv.shape[1:]
    has_x, has_y = has(flags, BEFORE_X)[:, 0:128], has(flags, BEFORE_Z)[:, 0:128]
    more = has(flags, AFTER_Z)[:, 0:128]
    low, high = below.shape[0] - 24, above.shape[0] - 40
    cs_near[...] = cs[...]
    cm_near[...] = cm[...]
    xsend[...] = jnp.zeros_like(xsend)
    next_rows[3 * nx :, :] = jnp.zeros_like(next_rows[3 * nx :, :])

    def ahead(field, x):
        at = high + field * nx + x
        return jnp.where(more, above[at : at + 1, 0:128], 0.0)

    for x in range(nx):
        here = [cs[c, x] for c in COARSE_S]
        here_row = [ahead(3 + c, x) for c in COARSE_S]
        if x == 0:
            before, before_row = [], []
            for k in range(3):
                at = 96 + 8 * k
                plane = jnp.concatenate([xr[at : at + 8, 0:128], xr[at : at + 8, 128:256]], axis=0)
                before.append(jnp.where(has_x, plane, 0.0))
                before_row.append(jnp.where(has_x, xr[120 + k : 121 + k, 0:128], 0.0))
        else:
            before = [cs[c, x - 1] for c in (0, 3, 4)]
            before_row = [ahead(3 + c, x - 1) for c in (0, 3, 4)]
        rows = [jnp.where(has_y, below[low + k * nx + x : low + k * nx + x + 1, 0:128], 0.0) for k in range(3)]
        new = velocity_plane([cv[c, x] for c in COARSE_V], here, before, rows, cm[0, x])
        last = [here[k][ny - 1 : ny] for k in (3, 1, 5)]
        old_row = [ahead(c, x) for c in COARSE_V]
        new_row = velocity_plane(old_row, here_row, before_row, last, ahead(9, x), lambda a, edge: edge)
        for c in range(3):
            out[c, x] = new[c]
            next_rows[c * nx + x : c * nx + x + 1, :] = new_row[c]
            if x == 0:
                xsend[8 * c : 8 * c + 8, 0:128] = new[c][0:8]
                xsend[8 * c : 8 * c + 8, 128:256] = new[c][8:16]
    for f in range(2):
        xsend[24 + f : 25 + f, 0:128] = rows_ref[f, 0:1, :].astype(F32)


def coarse_stress_kernel(cv, cs, cm, xr, zr, rows_ref, rest, rest_next, flags, _, v_out, s_out):
    nx, ny, nz = cv.shape[1:]
    base = xr.shape[0] - 32
    has_x, has_y = has(flags, AFTER_X)[:, 0:128], has(flags, AFTER_Z)[:, 0:128]
    row_ids = own_rows(flags, (ny, nz))

    def inserted(plane, c, x):
        for f in range(2):
            if x < nx:
                hit = row_ids == rows_ref[f, x : x + 1, :].astype(F32)
            else:
                hit = row_ids == xr[base + 24 + f : base + 25 + f, 0:128]
            at = (f * 3 + c) * nx + x % nx
            value = rest[at : at + 1, :] if x < nx else rest_next[at : at + 1, :]
            plane = jnp.where(hit, value, plane)
        return plane

    planes = [[inserted(cv[c, x], c, x) for c in range(3)] for x in range(nx)]
    edge = []
    for c in range(3):
        at = base + 8 * c
        plane = jnp.concatenate([xr[at : at + 8, 0:128], xr[at : at + 8, 128:256]], axis=0)
        edge.append(jnp.where(has_x, inserted(plane, c, nx), 0.0))
    planes.append(edge)
    for x in range(nx):
        for c in range(3):
            v_out[c, x] = planes[x][c]
        rows = [jnp.where(has_y, zr[k * nx + x : k * nx + x + 1, :], 0.0) for k in range(3)]
        new = stress_plane([cs[c, x] for c in COARSE_S], planes[x], planes[x + 1], rows, cm[1, x], cm[2, x])
        for c in range(6):
            s_out[c, x] = new[c]


def swap(value, axis, bit):
    count = lax.axis_size(axis)
    return lax.ppermute(value, axis, [(i, i ^ bit) for i in range(count)])


PARTNERS = ((2, (1, 3, 0, 4), (6, 5, 7)), (5, (4, 6, 7, 3), (2, 0, 1)))


def far(value, out):
    parts = []
    for turn in range(4):
        pairs = []
        for home, *lists in PARTNERS:
            for core, chips in enumerate(lists):
                if turn < len(chips):
                    pair = (2 * home + core, 2 * chips[turn] + core)
                    pairs.append(pair if out else pair[::-1])
        parts.append(lax.ppermute(value, "gy", pairs))
    return parts


def body(
    coarse_velocity,
    coarse_stress,
    coarse_material,
    fine_velocity,
    fine_stress,
    fine_material,
    fault_slip,
    initial_shear,
    normal_stress,
    fault_mask,
    zone_ids,
    static_friction,
    friction_drop,
    weakening_distance,
    owner_rows,
):
    nx, nz, ny = fine_velocity.shape[1:]
    cx, cy, cz = coarse_velocity.shape[1:]
    flags = make_flags(nz // 3, cy)
    shares = (6 * cx, cz)
    fault = (fault_slip, initial_shear, normal_stress, fault_mask, zone_ids)
    fields = (fine_velocity, fine_stress, fine_material)
    zoned = (static_friction, friction_drop, weakening_distance)
    given = [
        pltpu.with_memory_space_constraint(a, pltpu.HBM)
        for a in fields + (coarse_stress, coarse_velocity, coarse_material) + fault + zoned + (owner_rows,)
    ]
    up, down, raw = pl.pallas_call(
        pack_kernel,
        out_shape=[
            jax.ShapeDtypeStruct(shape, F32) for shape in ((nx * 32 + 24, ny), (nx * 40 + 48, ny), (nz, 128))
        ],
        in_specs=[HBM] * 14 + [VMEM],
        out_specs=[VMEM] * 3,
        scratch_shapes=[pltpu.VMEM((a.shape[0], nx, 8, ny), F32) for a in fields * 2]
        + [pltpu.VMEM((c, cx, 8, cz), F32) for c in (3, 3, 6)]
        + [pltpu.VMEM((cx, 8, cz), F32)]
        + [pltpu.SMEM(a.shape, F32) for a in zoned]
        + [pltpu.VMEM(a.shape, a.dtype) for a in fault]
        + [pltpu.VMEM((128, 128), F32), pltpu.SemaphoreType.DMA((20,))],
        compiler_params=PARAMS,
    )(*given[:14], flags)
    coupling = pl.pallas_call(
        coupling_kernel,
        out_shape=jax.ShapeDtypeStruct(shares, F32),
        in_specs=[HBM] * 2 + [VMEM] * 2,
        out_specs=VMEM,
        scratch_shapes=[
            pltpu.VMEM(coarse_velocity.shape, F32),
            pltpu.VMEM(owner_rows.shape, jnp.int32),
            pltpu.SemaphoreType.DMA((2,)),
        ],
        compiler_params=PARAMS,
    )(given[4], given[14], flags, raw)
    from_below, from_above = ring(up, "gy", 1), ring(down, "gy", -1)
    parts = far(coupling + swap(coupling, "gy", 1), True)
    rim, xsend, settings = call(
        rim_kernel,
        [(12, nx, RIM, ny), (208, ny), (7, 32, 128)],
        [VMEM] * 7,
        from_below, from_above, fine_stress, fine_material, coarse_stress, raw, flags,
    )
    slip = settings[0]
    xr = ring(xsend, "gx", 1)
    bounds = coupling + parts[0] + parts[1] + parts[2] + parts[3]
    bounds = (bounds, swap(bounds, "gy", 1))
    coarse_moved, cxs, coarse_zr, coarse_stress, coarse_material = call(
        coarse_velocity_kernel,
        [coarse_velocity.shape, (32, ny), (16, cz), coarse_stress.shape, coarse_material.shape],
        [VMEM] * 8,
        coarse_velocity, coarse_stress, coarse_material, xr, from_below, from_above, owner_rows, flags,
    )
    velocity, stress = fine_velocity, fine_stress

    def velocity_half(step, behind, *to_send):
        args = (velocity, stress, fine_material, rim, behind, *bounds, flags)
        sends = call(
            lambda *refs: velocity_edge_kernel(step, *refs),
            [(96, ny), (96, ny)] if step == 0 else [(128, ny), (96, ny)] if step == 1 else [(72, ny)],
            [VMEM] * (8 + len(to_send)), *args, *to_send,
        )
        moved = [ring(send, "gx", way) for send, way in zip(sends, (-1, 1))]
        (new,) = call(fine_velocity_kernel, [(3, nx, 32, ny)], [VMEM] * 8, *args)
        return new, moved

    def stress_half(step, xr, *more):
        return call(
            lambda *refs: fine_stress_kernel(step, *refs),
            [(6, nx, 32, ny), (32, 128), (96, ny), (32, 128)][: 4 - step], [VMEM] * (8 + len(more)),
            stress, velocity, fine_material, rim, xr, settings, slip, flags, *more,
        )

    given_behind = xr
    velocity, (xr, v_behind) = velocity_half(0, given_behind)
    stress, slip, behind, slip_behind = stress_half(0, xr, v_behind, given_behind)
    velocity, (coarse_xr, v_behind) = velocity_half(1, behind, cxs)
    stress, slip, behind = stress_half(1, coarse_xr, v_behind, given_behind, behind, slip_behind)
    (share,) = call(share_kernel, [shares], [VMEM] * 7, velocity, stress, fine_material, behind, *bounds, flags)
    share = share + swap(share, "gy", 1)
    velocity, (xr,) = velocity_half(2, behind)
    share, velocity = lax.optimization_barrier((share, velocity))
    parts = far(share, False)
    rest = parts[0] + parts[1] + parts[2] + parts[3]
    restricted = share + rest + swap(rest, "gy", 1)
    restricted_next = ring(restricted, "gx", -1)
    stress, velocity, slip, mark = pl.pallas_call(
        lambda *refs: fine_stress_kernel(2, *refs),
        out_shape=[jax.ShapeDtypeStruct(a.shape, F32) for a in (fine_stress, fine_velocity, fault_slip, raw[0:8])],
        in_specs=[VMEM] * 8,
        out_specs=[pl.BlockSpec(memory_space=pl.ANY)] * 2 + [VMEM] * 2,
        scratch_shapes=[pltpu.VMEM((6, nx, 32, ny), F32), pltpu.SemaphoreType.DMA((2 * nx + 2,))],
        compiler_params=PARAMS,
    )(stress, velocity, fine_material, rim, xr, settings, slip, flags)
    coarse_next, coarse_stress_next = call(
        coarse_stress_kernel,
        [coarse_velocity.shape, coarse_stress.shape],
        [VMEM] * 10,
        coarse_moved, coarse_stress, coarse_material, coarse_xr, coarse_zr, owner_rows, restricted, restricted_next,
        flags, mark,
    )
    return (coarse_next, coarse_stress_next, velocity, stress, slip)


def solution(mesh):
    grid = P(None, "gx", "gy", None)
    plane = P("gx", "gy")
    return jax.shard_map(
        body,
        mesh=mesh,
        in_specs=(grid,) * 6 + (plane,) * 5 + (P(),) * 3 + (P(None, "gx", None),),
        out_specs=(grid,) * 4 + (plane,),
        check_vma=False,
    )
```

```python
import jax
import jax.numpy as jnp
from jax import lax
from jax.experimental import pallas as pl
from jax.experimental.pallas import tpu as pltpu
from jax.sharding import PartitionSpec as P

STEP_RATIO = 0.15
F32 = jnp.float32
FINE_S = (0, 2, 1, 4, 3, 5)
FINE_V = (0, 2, 1)
COARSE_S = (0, 1, 2, 3, 4, 5)
COARSE_V = (0, 1, 2)
VMEM = pl.BlockSpec(memory_space=pltpu.VMEM)
SMEM = pl.BlockSpec(memory_space=pltpu.SMEM)
HBM = pl.BlockSpec(memory_space=pltpu.HBM)
PARAMS = pltpu.CompilerParams(vmem_limit_bytes=8 * 1024 * 1024)


def call(kernel, outs, specs, *args):
    return pl.pallas_call(
        kernel,
        out_shape=tuple(jax.ShapeDtypeStruct(shape, F32) for shape in outs),
        in_specs=list(specs),
        out_specs=tuple(VMEM for _ in outs),
        compiler_params=PARAMS,
    )(*args)


def ring(value, axis, steps):
    count = lax.axis_size(axis)
    return lax.ppermute(value, axis, [(i, (i + steps) % count) for i in range(count)])


def iota(shape, along):
    return lax.broadcasted_iota(jnp.int32, shape, along)


def b_behind(a, edge):
    return jnp.where(iota(a.shape, 0) == 0, edge, pltpu.roll(a, 1, 0))


def b_ahead(a, edge):
    last = a.shape[0] - 1
    return jnp.where(iota(a.shape, 0) == last, edge, pltpu.roll(a, last, 0))


def l_behind(a):
    return jnp.where(iota(a.shape, 1) == 0, 0.0, pltpu.roll(a, 1, 1))


def l_ahead(a):
    last = a.shape[1] - 1
    return jnp.where(iota(a.shape, 1) == last, 0.0, pltpu.roll(a, last, 1))


def velocity_plane(v, s, s_prev, rows, buoyancy, b_back=b_behind, l_back=l_behind):
    xx, bb, ll, xb, xl, bl = s
    p_xx, p_xb, p_xl = s_prev
    r_xb, r_bb, r_bl = rows
    f_x = (xx - p_xx) + (xb - b_back(xb, r_xb)) + (xl - l_back(xl))
    f_b = (xb - p_xb) + (bb - b_back(bb, r_bb)) + (bl - l_back(bl))
    f_l = (xl - p_xl) + (bl - b_back(bl, r_bl)) + (ll - l_back(ll))
    scale = STEP_RATIO * buoyancy
    return (v[0] + scale * f_x, v[1] + scale * f_b, v[2] + scale * f_l)


def stress_plane(s, v, v_next, rows, lame, shear, b_fore=b_ahead, l_fore=l_ahead):
    vx, vb, vl = v
    nx, nb, nl = v_next
    rx, rb, rl = rows
    e_x = nx - vx
    e_b = b_fore(vb, rb) - vb
    e_l = l_fore(vl) - vl
    e_xb = (b_fore(vx, rx) - vx) + (nb - vb)
    e_xl = (l_fore(vx) - vx) + (nl - vl)
    e_bl = (b_fore(vl, rl) - vl) + (l_fore(vb) - vb)
    common = (STEP_RATIO * lame) * (e_x + e_b + e_l)
    one = STEP_RATIO * shear
    two = 2.0 * one
    return (
        s[0] + (common + two * e_x),
        s[1] + (common + two * e_b),
        s[2] + (common + two * e_l),
        s[3] + one * e_xb,
        s[4] + one * e_xl,
        s[5] + one * e_bl,
    )


BEFORE_X, AFTER_X, BEFORE_Z, AFTER_Z, FIRST_CELL, FIRST_ROW = range(6)


def make_flags(cells, rows):
    gx, gy = lax.axis_index("gx"), lax.axis_index("gy")
    last_x, last_y = lax.axis_size("gx") - 1, lax.axis_size("gy") - 1
    values = (gx > 0, gx < last_x, gy > 0, gy < last_y, gy * cells, gy * rows, gx, gy)
    values = jnp.stack([jnp.asarray(v).astype(F32) for v in values])
    return jnp.broadcast_to(values[:, None], (8, 256))


def has(flags, which):
    return flags[which : which + 1, :] > 0.5


def own_cells(flags, depth):
    shape = (depth, 128)
    row = iota(shape, 0)
    cell = iota(shape, 1) - jnp.where(row < 27, row // 3, -1)
    return cell.astype(F32) == flags[FIRST_CELL : FIRST_CELL + 1, 0:128]


def own_rows(flags, shape):
    return iota(shape, 0).astype(F32) + flags[FIRST_ROW : FIRST_ROW + 1, 0:128]


RIM = 8
EDGES = (0, 10, 11)


def part_of(field, refs):
    if field < 3:
        return refs[0], field
    if field < 9:
        return refs[1], field - 3
    return refs[2], field - 9


def coupling_kernel(cv, rows_hbm, flags, _, coupling, cv_buf, rows_ref, sem):
    cx, cy, cz = cv.shape[1:]
    moves = ((cv, cv_buf), (rows_hbm, rows_ref))
    copies = [pltpu.make_async_copy(src, dst, sem.at[i]) for i, (src, dst) in enumerate(moves)]
    for copy in copies:
        copy.start()
    for copy in copies:
        copy.wait()
    ids = own_rows(flags, (cy, cz))
    for f in range(2):
        for x in range(cx):
            here = ids == rows_ref[f, x : x + 1, :].astype(F32)
            for c in range(3):
                row = jnp.sum(jnp.where(here, cv_buf[c, x], 0.0), axis=0, keepdims=True)
                at = (f * 3 + c) * cx + x
                coupling[at : at + 1, :] = row


def pack_kernel(
    fv, fs, fm, cs, cv, cm, slip, shear, normal, mask, zone, static, drop, distance, _,
    up, down, raw,
    top_v, top_s, top_m, low_v, low_s, low_m, cz_buf, cv_low, cs_low, cm_low, static_buf, drop_buf, distance_buf, slip_buf, shear_buf, normal_buf, mask_buf, zone_buf, turn, sem,
):
    nx, nz, ny = fv.shape[1:]
    cx, cy, cz = cs.shape[1:]
    fault = (slip_buf, shear_buf, normal_buf, mask_buf, zone_buf)
    zoned = (static_buf, drop_buf, distance_buf)
    moves = list(zip((slip, shear, normal, mask, zone, static, drop, distance), fault + zoned))
    moves.append((cv.at[:, :, 0:8, :], cv_low))
    for k, c in enumerate((3, 1, 5)):
        moves.append((cs.at[c, :, cy - 8 : cy, :], cz_buf.at[k]))
    moves.append((cs.at[:, :, 0:8, :], cs_low))
    moves.append((cm.at[0, :, 0:8, :], cm_low))
    early = len(moves)
    for src, top, low in ((fv, top_v, low_v), (fs, top_s, low_s), (fm, top_m, low_m)):
        moves.append((src.at[:, :, nz - 8 : nz, :], top))
        moves.append((src.at[:, :, 0:8, :], low))
    copies = [pltpu.make_async_copy(src, dst, sem.at[i]) for i, (src, dst) in enumerate(moves)]
    for copy in copies:
        copy.start()
    for copy in copies[:early]:
        copy.wait()
    turn[...] = jnp.zeros_like(turn)
    for k, ref in enumerate(fault):
        turn[16 * k : 16 * k + nx, 0:nz] = ref[...].astype(F32)
    turned = turn[...].T[0:nz]
    zones = pltpu.roll(turned, 128 - 64, 1)
    group = iota(turned.shape, 1) // 16
    for k in range(3):
        value = jnp.zeros_like(turned)
        for zone_id in range(4):
            part = zoned[k][zone_id]
            if k == 2:
                part = 1.0 / jnp.full(turned.shape, part)
            value = jnp.where(zones == float(zone_id), part, value)
        turned = jnp.where(group == 5 + k, pltpu.roll(value, 16 * (5 + k), 1), turned)
    raw[...] = turned
    at = nx * 32
    up[at:, :] = jnp.zeros((24, ny), F32)
    for k in range(3):
        for x in range(cx):
            up[at + k * cx + x : at + k * cx + x + 1, 0:128] = cz_buf[k, x, 7:8]
    up[at + 16 : at + 24, 0:128] = turned[nz - 8 :]
    down[nx * 40 :, :] = jnp.zeros((48, ny), F32)
    down[nx * 40 : nx * 40 + 8, 0:128] = turned[0:8]
    for c in range(10):
        for x in range(cx):
            if c < 3:
                row = cv_low[c, x, 0:1]
            elif c < 9:
                row = cs_low[c - 3, x, 0:1]
            else:
                row = cm_low[x, 0:1]
            at = nx * 40 + 8 + c * cx + x
            down[at : at + 1, 0:128] = row
    for copy in copies[early:]:
        copy.wait()
    tops, lows = (top_v, top_s, top_m), (low_v, low_s, low_m)
    sub = iota((RIM, ny), 0)

    def rolled(tile, by):
        return pltpu.roll(tile, by % RIM, 0) if by % RIM else tile

    def step(x, _):
        def take(refs, field):
            ref, c = part_of(field, refs)
            return ref[c, x]

        for t in range(3):
            tile = rolled(take(tops, 4 * t), -6)
            for i in range(1, 4):
                tile = jnp.where(sub // 2 == i, rolled(take(tops, 4 * t + i), 2 * i - 6), tile)
            up[pl.ds(x * 32 + 8 * t, 8), :] = tile
        tile = rolled(take(tops, 3 + 2), -5)
        tile = jnp.where(sub == 1, rolled(take(tops, 3 + 4), -4), tile)
        tile = jnp.where(sub == 2, rolled(take(tops, 3 + 5), -3), tile)
        up[pl.ds(x * 32 + 24, 8), :] = tile
        for t in range(5):
            tile = jnp.where(sub < 3, take(lows, 2 * t), rolled(take(lows, 2 * t + 1), 3))
            if t < 2:
                tile = jnp.where(sub < 6, tile, rolled(take(lows, 10 + t), 6))
            down[pl.ds(x * 40 + 8 * t, 8), :] = tile
        return 0

    lax.fori_loop(0, nx, step, 0)


def add_up(parts):
    total = parts[0][...]
    for part in parts[1:]:
        total = total + part[...]
    return total


def fault_settings(turned):
    return [turned] + [pltpu.roll(turned, 128 - 16 * k, 1) for k in (1, 2, 3, 5, 6, 7)]


def rim_kernel(from_below, from_above, fs, fm, cs, raw, flags, rim, xsend, settings):
    nx, nz, ny = fs.shape[1:]
    cx = cs.shape[1]
    has_below, has_above = has(flags, BEFORE_Z), has(flags, AFTER_Z)
    sub = iota((RIM, ny), 0)

    def rolled(tile, by):
        return pltpu.roll(tile, by % RIM, 0) if by % RIM else tile

    def step(x, _):
        last = jnp.where(has_below, from_below[pl.ds(x * 32 + 24, 8), :], 0.0)
        for t in range(3):
            tile = jnp.where(has_below, from_below[pl.ds(x * 32 + 8 * t, 8), :], 0.0)
            for i in range(4):
                field = 4 * t + i
                below = rolled(tile, 6 - 2 * i)
                extra = {5: 5, 7: 4, 8: 3}.get(field)
                if extra is not None:
                    below = jnp.where(sub == 5, rolled(last, extra), below)
                t2, i2 = divmod(field, 2)
                if field < 10:
                    above = from_above[pl.ds(x * 40 + 8 * t2, 8), :]
                    above = rolled(above, -3 * i2)
                else:
                    above = rolled(from_above[pl.ds(x * 40 + 8 * (field - 10), 8), :], 2)
                above = jnp.where(has_above, above, 0.0)
                rim[field, x] = jnp.where(sub < 4, above, below)
        return 0

    lax.fori_loop(0, nx, step, 0)
    for k, c in enumerate((0, 4, 3)):
        xsend[32 * k : 32 * k + nz, :] = fs[c, nx - 1]
        xsend[32 * k + nz : 32 * k + 32, :] = rim[3 + c, nx - 1]
    for k, c in enumerate((0, 3, 4)):
        xsend[96 + 8 * k : 104 + 8 * k, 0:128] = cs[c, cx - 1, 0:8]
        xsend[96 + 8 * k : 104 + 8 * k, 128:256] = cs[c, cx - 1, 8:16]
    xsend[120:128, :] = jnp.zeros((8, ny), F32)
    for k, c in enumerate((0, 3, 4)):
        at = nx * 40 + 8 + (3 + c) * cx + cx - 1
        xsend[120 + k : 121 + k, 0:128] = jnp.where(has_above[:, 0:128], from_above[at : at + 1, 0:128], 0.0)
    below = jnp.where(has_below[:, 0:128], from_below[nx * 32 + 16 :, 0:128], 0.0)
    above = jnp.where(has_above[:, 0:128], from_above[nx * 40 : nx * 40 + 8, 0:128], 0.0)
    turned = jnp.concatenate([raw[...], jnp.where(iota((RIM, 128), 0) < 4, above, below)], axis=0)
    for k in (1, 2):
        at = 96 + 32 * k
        xsend[at : at + nz, :] = fm[k, nx - 1]
        xsend[at + nz : at + 32, :] = rim[9 + k, nx - 1]
    xsend[192:208, 0:128] = turned[0:16]
    xsend[192:208, 128:256] = turned[16:32]
    for k, part in enumerate(fault_settings(turned)):
        settings[k] = part


def ring_back(a, _):
    return pltpu.roll(a, 1, 0)


def ring_fore(a, _):
    return pltpu.roll(a, a.shape[0] - 1, 0)


def reader(ref, rim, first):
    if ref.shape[1] == len(EDGES):
        return lambda c, x: ref[c, EDGES.index(x)]
    if ref.shape[2] == 32:
        return lambda c, x: ref[c, x]
    return lambda c, x: jnp.concatenate([ref[c, x], rim[first + c, x]], axis=0)


def held_column(bounds, cells, face, c, x):
    at = (face * 3 + c) * (bounds.shape[0] // 6) + x
    return jnp.sum(jnp.where(cells, bounds[at : at + 1, :], 0.0), axis=1, keepdims=True)


def held(value, columns):
    lane = iota(value.shape, 1)
    value = jnp.where(lane == 0, columns[0], value)
    return jnp.where(lane == value.shape[1] - 1, columns[1], value)


def merged(a):
    return jnp.where(iota((a.shape[0], 128), 1) < 64, a[:, 0:128], a[:, a.shape[1] - 128 :])


def velocity_planes(planes, v_ref, s_ref, m_ref, rim, behind, bounds_a, bounds_b, flags, put):
    bounds = bounds_a[...] + bounds_b[...]
    v, s, m = reader(v_ref, rim, 0), reader(s_ref, rim, 3), reader(m_ref, rim, 9)
    nz = 32
    cells = own_cells(flags, nz)
    has_x = has(flags, BEFORE_X)
    columns = {}
    for x in planes:
        here = [s(c, x) for c in FINE_S]
        if x // 3 not in columns:
            columns[x // 3] = [[held_column(bounds, cells, f, c, x // 3) for f in range(2)] for c in range(3)]
        if x == 0:
            before = [jnp.where(has_x, behind[k * nz : (k + 1) * nz, :], 0.0) for k in range(3)]
        else:
            before = [s(c, x - 1) for c in (0, 4, 3)]
        old = [v(c, x) for c in FINE_V]
        new = velocity_plane(old, here, before, (0.0,) * 3, m(0, x), ring_back)
        put(x, [held(new[k], columns[x // 3][c]) for k, c in enumerate(FINE_V)])


def velocity_edge_kernel(step, v, s, m, rim, behind, bounds_a, bounds_b, flags, *refs):
    refs = list(refs)
    more = [refs.pop(0)] if step == 1 else []
    nz = 32 if step < 2 else 24

    def put(x, new):
        for k in range(3):
            refs[0 if x == 0 else 1][k * nz : (k + 1) * nz, :] = new[k][0:nz]

    planes = [0] if step == 2 else [0, v.shape[1] - 1]
    velocity_planes(planes, v, s, m, rim, behind, bounds_a, bounds_b, flags, put)
    if step == 1:
        refs[0][3 * nz :, :] = more[0][...]


def fine_velocity_kernel(v, s, m, rim, behind, bounds_a, bounds_b, flags, out):
    def put(x, new):
        for k, c in enumerate(FINE_V):
            out[c, x] = new[k]

    velocity_planes(range(v.shape[1]), v, s, m, rim, behind, bounds_a, bounds_b, flags, put)


def share_kernel(v, s, m, behind, bounds_a, bounds_b, flags, share):
    nx, nz, ny = v.shape[1:]
    cx, own = nx // 3, nz - RIM
    bounds = bounds_a[...] + bounds_b[...]
    lane = iota((own, 128), 1)
    cells = own_cells(flags, own)

    def l_back(a):
        return pltpu.roll(a, 1, 1)

    columns = [[[held_column(bounds, cells, f, c, x) for f in range(2)] for c in range(3)] for x in range(cx)]
    sums = {}
    before = [merged(behind[k * nz : k * nz + own, :]) for k in range(3)]
    for x in range(nx):
        here = [merged(s[c, x]) for c in FINE_S]
        old = [merged(v[c, x, 0:own, :]) for c in FINE_V]
        rows = [here[k][nz - 1 : nz] for k in (3, 1, 5)]
        here = [a[0:own] for a in here]
        new = velocity_plane(old, here, before, rows, merged(m[0, x]), b_behind, l_back)
        before = [here[0], here[3], here[4]]
        for k, c in enumerate(FINE_V):
            val = held(new[k], columns[x // 3][c])
            sums[c, x // 3] = val if x % 3 == 0 else sums[c, x // 3] + val
    for f in range(2):
        face = lane < 3 if f == 0 else lane >= 125
        for c in range(3):
            for x in range(cx):
                at = (f * 3 + c) * cx + x
                total = jnp.sum(jnp.where(face, sums[c, x], 0.0), axis=1, keepdims=True)
                row = jnp.sum(jnp.where(cells, total, 0.0), axis=0, keepdims=True)
                share[at : at + 1, :] = row * (1.0 / 27.0)


def stress_planes(planes, s_ref, v_ref, m_ref, rim, xr, flags, put):
    v, s, m = reader(v_ref, rim, 0), reader(s_ref, rim, 3), reader(m_ref, rim, 9)
    nx, nz, half = s_ref.shape[1], 32, s_ref.shape[3] // 2
    has_x = has(flags, AFTER_X)
    lane = iota((nz, 128), 1)
    shear_plane = jnp.zeros((nz, 128), F32)
    for x in planes:
        here = [v(c, x) for c in FINE_V]
        if x == nx - 1:
            rows = nz if xr.shape[0] >= 3 * nz else nz - RIM
            after = [jnp.where(has_x, xr[k * rows : (k + 1) * rows, :], 0.0) for k in range(3)]
            if rows < nz:
                rest = jnp.zeros((nz - rows, xr.shape[1]), F32)
                after = [jnp.concatenate([plane, rest], axis=0) for plane in after]
        else:
            after = [v(c, x + 1) for c in FINE_V]
        old = [s(c, x) for c in FINE_S]
        new = stress_plane(old, here, after, (0.0,) * 3, m(1, x), m(2, x), ring_fore)
        put(x, new)
        moved = new[4][:, half : half + 128]
        moved = moved if x == 0 else pltpu.roll(moved, x, 1)
        shear_plane = jnp.where(lane == x, moved, shear_plane)
    return shear_plane


def friction(shear_plane, settings, old):
    traction = shear_plane + settings[1]
    weakened = jnp.minimum(old * settings[6], 1.0)
    strength = settings[2] * (settings[4] - settings[5] * weakened)
    resisted = jnp.clip(traction, -strength, strength)
    active = settings[3]
    fresh = old + active * STEP_RATIO * jnp.abs(traction - resisted)
    return fresh, shear_plane + active * (resisted - traction)


def with_fault(upper, fixed, x):
    moved = fixed if x == 0 else pltpu.roll(fixed, 128 - x, 1)
    return jnp.where(iota(upper.shape, 1) == 0, moved, upper)


def stress_behind(old, v_behind, v_first, given, slip, flags, out, slip_out):
    nz, half = 32, v_behind.shape[1] // 2
    has_x = has(flags, BEFORE_X)
    here = [v_behind[k * nz : (k + 1) * nz, :] for k in range(3)]
    xx, xb, xl = (old[k * nz : (k + 1) * nz, :] for k in range(3))
    lame, shear = given[128:160, :], given[160:192, :]
    new = stress_plane((xx, xx, xx, xb, xl, xl), here, v_first, (0.0,) * 3, lame, shear, ring_fore)
    turned = jnp.concatenate([given[192:208, 0:128], given[192:208, 128:256]], axis=0)
    settings = fault_settings(turned)
    last = 11
    xl = new[4]
    before = settings[0] if slip is None else slip[...]
    fresh, fixed = friction(pltpu.roll(xl[:, half : half + 128], last, 1), settings, before)
    if slip_out is not None:
        slip_out[...] = fresh
    xl = jnp.concatenate([xl[:, 0:half], with_fault(xl[:, half:], fixed, last)], axis=1)
    for k, value in enumerate((new[0], new[3], xl)):
        out[k * nz : (k + 1) * nz, :] = jnp.where(has_x, value, 0.0)


def stress_edge_kernel(s, v, m, rim, xr, settings, slip, flags, v_behind, given, out, behind, slip_behind):
    half = s.shape[3] // 2
    stress_behind(given, v_behind, [v[c, 0] for c in FINE_V], given, None, flags, behind, slip_behind)

    def put(x, new):
        for k, c in enumerate(FINE_S):
            out[c, EDGES.index(x)] = new[k]

    shear_plane = stress_planes(EDGES, s, v, m, rim, xr, flags, put)
    _, fixed = friction(shear_plane, settings, slip[...])
    for at, x in enumerate(EDGES):
        out[3, at, :, half:] = with_fault(out[3, at, :, half:], fixed, x)


def fine_stress_kernel(step, s, v, m, rim, xr, settings, slip, flags, *refs):
    last = step == 2
    copies = []
    nx, nz, half = s.shape[1], 32, s.shape[3] // 2
    own = nz - RIM
    if last:
        final, v_final, slip_out, mark, out, sem = refs
        mark[...] = jnp.zeros_like(mark)
        copies.append(pltpu.make_async_copy(v.at[:, :, 0:own, :], v_final, sem.at[0]))
        copies[0].start()
    else:
        if step == 1:
            v_behind, given, old, slip_before, out, slip_out, behind = refs
            first = [v[c, 0] for c in FINE_V]
            stress_behind(old, v_behind, first, given, slip_before, flags, behind, None)
        else:
            out, slip_out = refs

    def put(x, new):
        for k, c in enumerate(FINE_S):
            out[c, x] = new[k]
        if last:
            for first, end in ((0, 3), (4, 6)):
                at = len(copies)
                copies.append(
                    pltpu.make_async_copy(out.at[first:end, x, 0:own, :], final.at[first:end, x], sem.at[at])
                )
                copies[at].start()

    shear_plane = stress_planes(range(nx), s, v, m, rim, xr, flags, put)
    fresh, fixed = friction(shear_plane, settings, slip[...])
    for x in range(nx):
        out[3, x, :, half:] = with_fault(out[3, x, :, half:], fixed, x)
    if last:
        copies.append(pltpu.make_async_copy(out.at[3, :, 0:own, :], final.at[3], sem.at[len(copies)]))
        copies[-1].start()
        turned = jnp.concatenate([fresh, jnp.zeros((128 - nz, 128), F32)], axis=0).T
        slip_out[...] = turned[0:nx, 0:own]
        for copy in copies:
            copy.wait()
    else:
        slip_out[...] = fresh


def coarse_velocity_kernel(cv, cs, cm, xr, below, above, rows_ref, flags, out, xsend, next_rows, cs_near, cm_near):
    nx, ny, nz = cv.shape[1:]
    has_x, has_y = has(flags, BEFORE_X)[:, 0:128], has(flags, BEFORE_Z)[:, 0:128]
    more = has(flags, AFTER_Z)[:, 0:128]
    low, high = below.shape[0] - 24, above.shape[0] - 40
    cs_near[...] = cs[...]
    cm_near[...] = cm[...]
    xsend[...] = jnp.zeros_like(xsend)
    next_rows[3 * nx :, :] = jnp.zeros_like(next_rows[3 * nx :, :])

    def ahead(field, x):
        at = high + field * nx + x
        return jnp.where(more, above[at : at + 1, 0:128], 0.0)

    for x in range(nx):
        here = [cs[c, x] for c in COARSE_S]
        here_row = [ahead(3 + c, x) for c in COARSE_S]
        if x == 0:
            before, before_row = [], []
            for k in range(3):
                at = 96 + 8 * k
                plane = jnp.concatenate([xr[at : at + 8, 0:128], xr[at : at + 8, 128:256]], axis=0)
                before.append(jnp.where(has_x, plane, 0.0))
                before_row.append(jnp.where(has_x, xr[120 + k : 121 + k, 0:128], 0.0))
        else:
            before = [cs[c, x - 1] for c in (0, 3, 4)]
            before_row = [ahead(3 + c, x - 1) for c in (0, 3, 4)]
        rows = [jnp.where(has_y, below[low + k * nx + x : low + k * nx + x + 1, 0:128], 0.0) for k in range(3)]
        new = velocity_plane([cv[c, x] for c in COARSE_V], here, before, rows, cm[0, x])
        last = [here[k][ny - 1 : ny] for k in (3, 1, 5)]
        old_row = [ahead(c, x) for c in COARSE_V]
        new_row = velocity_plane(old_row, here_row, before_row, last, ahead(9, x), lambda a, edge: edge)
        for c in range(3):
            out[c, x] = new[c]
            next_rows[c * nx + x : c * nx + x + 1, :] = new_row[c]
            if x == 0:
                xsend[8 * c : 8 * c + 8, 0:128] = new[c][0:8]
                xsend[8 * c : 8 * c + 8, 128:256] = new[c][8:16]
    for f in range(2):
        xsend[24 + f : 25 + f, 0:128] = rows_ref[f, 0:1, :].astype(F32)


def coarse_stress_kernel(cv, cs, cm, xr, zr, rows_ref, rest, rest_next, flags, _, v_out, s_out):
    nx, ny, nz = cv.shape[1:]
    base = xr.shape[0] - 32
    has_x, has_y = has(flags, AFTER_X)[:, 0:128], has(flags, AFTER_Z)[:, 0:128]
    row_ids = own_rows(flags, (ny, nz))

    def inserted(plane, c, x):
        for f in range(2):
            if x < nx:
                hit = row_ids == rows_ref[f, x : x + 1, :].astype(F32)
            else:
                hit = row_ids == xr[base + 24 + f : base + 25 + f, 0:128]
            at = (f * 3 + c) * nx + x % nx
            value = rest[at : at + 1, :] if x < nx else rest_next[at : at + 1, :]
            plane = jnp.where(hit, value, plane)
        return plane

    planes = [[inserted(cv[c, x], c, x) for c in range(3)] for x in range(nx)]
    edge = []
    for c in range(3):
        at = base + 8 * c
        plane = jnp.concatenate([xr[at : at + 8, 0:128], xr[at : at + 8, 128:256]], axis=0)
        edge.append(jnp.where(has_x, inserted(plane, c, nx), 0.0))
    planes.append(edge)
    for x in range(nx):
        for c in range(3):
            v_out[c, x] = planes[x][c]
        rows = [jnp.where(has_y, zr[k * nx + x : k * nx + x + 1, :], 0.0) for k in range(3)]
        new = stress_plane([cs[c, x] for c in COARSE_S], planes[x], planes[x + 1], rows, cm[1, x], cm[2, x])
        for c in range(6):
            s_out[c, x] = new[c]


def swap(value, axis, bit):
    count = lax.axis_size(axis)
    return lax.ppermute(value, axis, [(i, i ^ bit) for i in range(count)])


def apart(value, out):
    parts = []
    for turn in range(1, 8):
        pairs = [(home, 2 * ((home // 2 + turn) % 8) + home % 2) for home in (5, 10)]
        parts.append(lax.ppermute(value, "gy", [pair if out else pair[::-1] for pair in pairs]))
    return parts


def body(
    coarse_velocity,
    coarse_stress,
    coarse_material,
    fine_velocity,
    fine_stress,
    fine_material,
    fault_slip,
    initial_shear,
    normal_stress,
    fault_mask,
    zone_ids,
    static_friction,
    friction_drop,
    weakening_distance,
    owner_rows,
):
    nx, nz, ny = fine_velocity.shape[1:]
    cx, cy, cz = coarse_velocity.shape[1:]
    flags = make_flags(nz // 3, cy)
    shares = (6 * cx, cz)
    fault = (fault_slip, initial_shear, normal_stress, fault_mask, zone_ids)
    fields = (fine_velocity, fine_stress, fine_material)
    zoned = (static_friction, friction_drop, weakening_distance)
    given = [
        pltpu.with_memory_space_constraint(a, pltpu.HBM)
        for a in fields + (coarse_stress, coarse_velocity, coarse_material) + fault + zoned + (owner_rows,)
    ]
    up, down, raw = pl.pallas_call(
        pack_kernel,
        out_shape=[
            jax.ShapeDtypeStruct(shape, F32) for shape in ((nx * 32 + 24, ny), (nx * 40 + 48, ny), (nz, 128))
        ],
        in_specs=[HBM] * 14 + [VMEM],
        out_specs=[VMEM] * 3,
        scratch_shapes=[pltpu.VMEM((a.shape[0], nx, 8, ny), F32) for a in fields * 2]
        + [pltpu.VMEM((c, cx, 8, cz), F32) for c in (3, 3, 6)]
        + [pltpu.VMEM((cx, 8, cz), F32)]
        + [pltpu.SMEM(a.shape, F32) for a in zoned]
        + [pltpu.VMEM(a.shape, a.dtype) for a in fault]
        + [pltpu.VMEM((128, 128), F32), pltpu.SemaphoreType.DMA((20,))],
        compiler_params=PARAMS,
    )(*given[:14], flags)
    coupling = pl.pallas_call(
        coupling_kernel,
        out_shape=jax.ShapeDtypeStruct(shares, F32),
        in_specs=[HBM] * 2 + [VMEM] * 2,
        out_specs=VMEM,
        scratch_shapes=[
            pltpu.VMEM(coarse_velocity.shape, F32),
            pltpu.VMEM(owner_rows.shape, jnp.int32),
            pltpu.SemaphoreType.DMA((2,)),
        ],
        compiler_params=PARAMS,
    )(given[4], given[14], flags, raw)
    from_below, from_above = ring(up, "gy", 1), ring(down, "gy", -1)
    parts = apart(coupling, True)
    rim, xsend, settings = call(
        rim_kernel,
        [(12, nx, RIM, ny), (208, ny), (7, 32, 128)],
        [VMEM] * 7,
        from_below, from_above, fine_stress, fine_material, coarse_stress, raw, flags,
    )
    slip = settings[0]
    xr = ring(xsend, "gx", 1)
    bounds = coupling + sum(parts[1:], parts[0])
    bounds = (bounds, swap(bounds, "gy", 1))
    coarse_moved, cxs, coarse_zr, coarse_stress, coarse_material = call(
        coarse_velocity_kernel,
        [coarse_velocity.shape, (32, ny), (16, cz), coarse_stress.shape, coarse_material.shape],
        [VMEM] * 8,
        coarse_velocity, coarse_stress, coarse_material, xr, from_below, from_above, owner_rows, flags,
    )
    velocity, stress = fine_velocity, fine_stress

    def velocity_half(step, behind, *to_send):
        args = (velocity, stress, fine_material, rim, behind, *bounds, flags)
        near = (velocity, edges, *args[2:]) if step == 1 else args
        sends = call(
            lambda *refs: velocity_edge_kernel(step, *refs),
            [(96, ny), (96, ny)] if step == 0 else [(128, ny), (96, ny)] if step == 1 else [(72, ny)],
            [VMEM] * (8 + len(to_send) * (step < 2)), *near, *(to_send if step < 2 else ()),
        )
        sends = list(sends)
        if step == 2:
            sends[0], *to_send = lax.optimization_barrier((sends[0], *to_send))
        moved = [ring(send, "gx", way) for send, way in zip(sends, (-1, 1))]
        (new,) = call(fine_velocity_kernel, [(3, nx, 32, ny)], [VMEM] * 8, *args)
        return (new, moved, *to_send) if step == 2 else (new, moved)

    def stress_half(step, xr, *more):
        return call(
            lambda *refs: fine_stress_kernel(step, *refs),
            [(6, nx, 32, ny), (32, 128), (96, ny)][: 2 + step], [VMEM] * (8 + len(more)),
            stress, velocity, fine_material, rim, xr, settings, slip, flags, *more,
        )

    given_behind = xr
    velocity, (xr, v_behind) = velocity_half(0, given_behind)
    edges, behind, slip_behind = call(
        stress_edge_kernel, [(6, len(EDGES), 32, ny), (96, ny), (32, 128)], [VMEM] * 10,
        stress, velocity, fine_material, rim, xr, settings, slip, flags, v_behind, given_behind,
    )
    stress, slip = stress_half(0, xr)
    velocity, (coarse_xr, v_behind) = velocity_half(1, behind, cxs)
    stress, slip, behind = stress_half(1, coarse_xr, v_behind, given_behind, behind, slip_behind)
    (share,) = call(share_kernel, [shares], [VMEM] * 7, velocity, stress, fine_material, behind, *bounds, flags)
    share = share + swap(share, "gy", 1)
    velocity, (xr,), share = velocity_half(2, behind, share)
    parts = apart(share, False)
    restricted = share + sum(parts[1:], parts[0])
    restricted_next = ring(restricted, "gx", -1)
    stress, velocity, slip, mark = pl.pallas_call(
        lambda *refs: fine_stress_kernel(2, *refs),
        out_shape=[jax.ShapeDtypeStruct(a.shape, F32) for a in (fine_stress, fine_velocity, fault_slip, raw[0:8])],
        in_specs=[VMEM] * 8,
        out_specs=[pl.BlockSpec(memory_space=pl.ANY)] * 2 + [VMEM] * 2,
        scratch_shapes=[pltpu.VMEM((6, nx, 32, ny), F32), pltpu.SemaphoreType.DMA((2 * nx + 2,))],
        compiler_params=PARAMS,
    )(stress, velocity, fine_material, rim, xr, settings, slip, flags)
    coarse_next, coarse_stress_next = call(
        coarse_stress_kernel,
        [coarse_velocity.shape, coarse_stress.shape],
        [VMEM] * 10,
        coarse_moved, coarse_stress, coarse_material, coarse_xr, coarse_zr, owner_rows, restricted, restricted_next,
        flags, mark,
    )
    return (coarse_next, coarse_stress_next, velocity, stress, slip)


def solution(mesh):
    grid = P(None, "gx", "gy", None)
    plane = P("gx", "gy")
    return jax.shard_map(
        body,
        mesh=mesh,
        in_specs=(grid,) * 6 + (plane,) * 5 + (P(),) * 3 + (P(None, "gx", None),),
        out_specs=(grid,) * 4 + (plane,),
        check_vma=False,
    )
```

```python
import jax
import jax.numpy as jnp
from jax import lax
from jax.experimental import pallas as pl
from jax.experimental.pallas import tpu as pltpu
from jax.sharding import PartitionSpec as P

STEP_RATIO = 0.15
F32 = jnp.float32
FINE_S = (0, 2, 1, 4, 3, 5)
FINE_V = (0, 2, 1)
COARSE_S = (0, 1, 2, 3, 4, 5)
COARSE_V = (0, 1, 2)
VMEM = pl.BlockSpec(memory_space=pltpu.VMEM)
SMEM = pl.BlockSpec(memory_space=pltpu.SMEM)
HBM = pl.BlockSpec(memory_space=pltpu.HBM)
PARAMS = pltpu.CompilerParams(vmem_limit_bytes=8 * 1024 * 1024)


def call(kernel, outs, specs, *args):
    return pl.pallas_call(
        kernel,
        out_shape=tuple(jax.ShapeDtypeStruct(shape, F32) for shape in outs),
        in_specs=list(specs),
        out_specs=tuple(VMEM for _ in outs),
        compiler_params=PARAMS,
    )(*args)


def ring(value, axis, steps):
    count = lax.axis_size(axis)
    return lax.ppermute(value, axis, [(i, (i + steps) % count) for i in range(count)])


def iota(shape, along):
    return lax.broadcasted_iota(jnp.int32, shape, along)


def b_behind(a, edge):
    return jnp.where(iota(a.shape, 0) == 0, edge, pltpu.roll(a, 1, 0))


def b_ahead(a, edge):
    last = a.shape[0] - 1
    return jnp.where(iota(a.shape, 0) == last, edge, pltpu.roll(a, last, 0))


def l_behind(a):
    return jnp.where(iota(a.shape, 1) == 0, 0.0, pltpu.roll(a, 1, 1))


def l_ahead(a):
    last = a.shape[1] - 1
    return jnp.where(iota(a.shape, 1) == last, 0.0, pltpu.roll(a, last, 1))


def velocity_plane(v, s, s_prev, rows, buoyancy, b_back=b_behind, l_back=l_behind):
    xx, bb, ll, xb, xl, bl = s
    p_xx, p_xb, p_xl = s_prev
    r_xb, r_bb, r_bl = rows
    f_x = (xx - p_xx) + (xb - b_back(xb, r_xb)) + (xl - l_back(xl))
    f_b = (xb - p_xb) + (bb - b_back(bb, r_bb)) + (bl - l_back(bl))
    f_l = (xl - p_xl) + (bl - b_back(bl, r_bl)) + (ll - l_back(ll))
    scale = STEP_RATIO * buoyancy
    return (v[0] + scale * f_x, v[1] + scale * f_b, v[2] + scale * f_l)


def stress_plane(s, v, v_next, rows, lame, shear, b_fore=b_ahead, l_fore=l_ahead):
    vx, vb, vl = v
    nx, nb, nl = v_next
    rx, rb, rl = rows
    e_x = nx - vx
    e_b = b_fore(vb, rb) - vb
    e_l = l_fore(vl) - vl
    e_xb = (b_fore(vx, rx) - vx) + (nb - vb)
    e_xl = (l_fore(vx) - vx) + (nl - vl)
    e_bl = (b_fore(vl, rl) - vl) + (l_fore(vb) - vb)
    common = (STEP_RATIO * lame) * (e_x + e_b + e_l)
    one = STEP_RATIO * shear
    two = 2.0 * one
    return (
        s[0] + (common + two * e_x),
        s[1] + (common + two * e_b),
        s[2] + (common + two * e_l),
        s[3] + one * e_xb,
        s[4] + one * e_xl,
        s[5] + one * e_bl,
    )


BEFORE_X, AFTER_X, BEFORE_Z, AFTER_Z, FIRST_CELL, FIRST_ROW = range(6)


def make_flags(cells, rows):
    gx, gy = lax.axis_index("gx"), lax.axis_index("gy")
    last_x, last_y = lax.axis_size("gx") - 1, lax.axis_size("gy") - 1
    values = (gx > 0, gx < last_x, gy > 0, gy < last_y, gy * cells, gy * rows, gx, gy)
    values = jnp.stack([jnp.asarray(v).astype(F32) for v in values])
    return jnp.broadcast_to(values[:, None], (8, 256))


def has(flags, which):
    return flags[which : which + 1, :] > 0.5


def own_cells(flags, depth):
    shape = (depth, 128)
    row = iota(shape, 0)
    cell = iota(shape, 1) - jnp.where(row < 27, row // 3, -1)
    return cell.astype(F32) == flags[FIRST_CELL : FIRST_CELL + 1, 0:128]


def own_rows(flags, shape):
    return iota(shape, 0).astype(F32) + flags[FIRST_ROW : FIRST_ROW + 1, 0:128]


RIM = 8
EDGES = (0, 10, 11)


def part_of(field, refs):
    if field < 3:
        return refs[0], field
    if field < 9:
        return refs[1], field - 3
    return refs[2], field - 9


def coupling_kernel(cv, rows_hbm, flags, _, coupling, cv_buf, rows_ref, sem):
    cx, cy, cz = cv.shape[1:]
    moves = ((cv, cv_buf), (rows_hbm, rows_ref))
    copies = [pltpu.make_async_copy(src, dst, sem.at[i]) for i, (src, dst) in enumerate(moves)]
    for copy in copies:
        copy.start()
    for copy in copies:
        copy.wait()
    ids = own_rows(flags, (cy, cz))
    for f in range(2):
        for x in range(cx):
            here = ids == rows_ref[f, x : x + 1, :].astype(F32)
            for c in range(3):
                row = jnp.sum(jnp.where(here, cv_buf[c, x], 0.0), axis=0, keepdims=True)
                at = (f * 3 + c) * cx + x
                coupling[at : at + 1, :] = row


def pack_kernel(
    fv, fs, fm, cs, cv, cm, slip, shear, normal, mask, zone, static, drop, distance, _,
    up, down, raw,
    top_v, top_s, top_m, low_v, low_s, low_m, cz_buf, cv_low, cs_low, cm_low, static_buf, drop_buf, distance_buf, slip_buf, shear_buf, normal_buf, mask_buf, zone_buf, turn, sem,
):
    nx, nz, ny = fv.shape[1:]
    cx, cy, cz = cs.shape[1:]
    fault = (slip_buf, shear_buf, normal_buf, mask_buf, zone_buf)
    zoned = (static_buf, drop_buf, distance_buf)
    moves = list(zip((slip, shear, normal, mask, zone, static, drop, distance), fault + zoned))
    moves.append((cv.at[:, :, 0:8, :], cv_low))
    for k, c in enumerate((3, 1, 5)):
        moves.append((cs.at[c, :, cy - 8 : cy, :], cz_buf.at[k]))
    moves.append((cs.at[:, :, 0:8, :], cs_low))
    moves.append((cm.at[0, :, 0:8, :], cm_low))
    early = len(moves)
    for src, top, low in ((fv, top_v, low_v), (fs, top_s, low_s), (fm, top_m, low_m)):
        moves.append((src.at[:, :, nz - 8 : nz, :], top))
        moves.append((src.at[:, :, 0:8, :], low))
    copies = [pltpu.make_async_copy(src, dst, sem.at[i]) for i, (src, dst) in enumerate(moves)]
    for copy in copies:
        copy.start()
    for copy in copies[:early]:
        copy.wait()
    turn[...] = jnp.zeros_like(turn)
    for k, ref in enumerate(fault):
        turn[16 * k : 16 * k + nx, 0:nz] = ref[...].astype(F32)
    turned = turn[...].T[0:nz]
    zones = pltpu.roll(turned, 128 - 64, 1)
    group = iota(turned.shape, 1) // 16
    for k in range(3):
        value = jnp.zeros_like(turned)
        for zone_id in range(4):
            part = zoned[k][zone_id]
            if k == 2:
                part = 1.0 / jnp.full(turned.shape, part)
            value = jnp.where(zones == float(zone_id), part, value)
        turned = jnp.where(group == 5 + k, pltpu.roll(value, 16 * (5 + k), 1), turned)
    raw[...] = turned
    at = nx * 32
    up[at:, :] = jnp.zeros((24, ny), F32)
    for k in range(3):
        for x in range(cx):
            up[at + k * cx + x : at + k * cx + x + 1, 0:128] = cz_buf[k, x, 7:8]
    up[at + 16 : at + 24, 0:128] = turned[nz - 8 :]
    down[nx * 40 :, :] = jnp.zeros((48, ny), F32)
    down[nx * 40 : nx * 40 + 8, 0:128] = turned[0:8]
    for c in range(10):
        for x in range(cx):
            if c < 3:
                row = cv_low[c, x, 0:1]
            elif c < 9:
                row = cs_low[c - 3, x, 0:1]
            else:
                row = cm_low[x, 0:1]
            at = nx * 40 + 8 + c * cx + x
            down[at : at + 1, 0:128] = row
    for copy in copies[early:]:
        copy.wait()
    tops, lows = (top_v, top_s, top_m), (low_v, low_s, low_m)
    sub = iota((RIM, ny), 0)

    def rolled(tile, by):
        return pltpu.roll(tile, by % RIM, 0) if by % RIM else tile

    def step(x, _):
        def take(refs, field):
            ref, c = part_of(field, refs)
            return ref[c, x]

        for t in range(3):
            tile = rolled(take(tops, 4 * t), -6)
            for i in range(1, 4):
                tile = jnp.where(sub // 2 == i, rolled(take(tops, 4 * t + i), 2 * i - 6), tile)
            up[pl.ds(x * 32 + 8 * t, 8), :] = tile
        tile = rolled(take(tops, 3 + 2), -5)
        tile = jnp.where(sub == 1, rolled(take(tops, 3 + 4), -4), tile)
        tile = jnp.where(sub == 2, rolled(take(tops, 3 + 5), -3), tile)
        up[pl.ds(x * 32 + 24, 8), :] = tile
        for t in range(5):
            tile = jnp.where(sub < 3, take(lows, 2 * t), rolled(take(lows, 2 * t + 1), 3))
            if t < 2:
                tile = jnp.where(sub < 6, tile, rolled(take(lows, 10 + t), 6))
            down[pl.ds(x * 40 + 8 * t, 8), :] = tile
        return 0

    lax.fori_loop(0, nx, step, 0)


def add_up(parts):
    total = parts[0][...]
    for part in parts[1:]:
        total = total + part[...]
    return total


def fault_settings(turned):
    return [turned] + [pltpu.roll(turned, 128 - 16 * k, 1) for k in (1, 2, 3, 5, 6, 7)]


def rim_kernel(from_below, from_above, fs, fm, cs, raw, flags, rim, xsend, settings):
    nx, nz, ny = fs.shape[1:]
    cx = cs.shape[1]
    has_below, has_above = has(flags, BEFORE_Z), has(flags, AFTER_Z)
    sub = iota((RIM, ny), 0)

    def rolled(tile, by):
        return pltpu.roll(tile, by % RIM, 0) if by % RIM else tile

    def step(x, _):
        last = jnp.where(has_below, from_below[pl.ds(x * 32 + 24, 8), :], 0.0)
        for t in range(3):
            tile = jnp.where(has_below, from_below[pl.ds(x * 32 + 8 * t, 8), :], 0.0)
            for i in range(4):
                field = 4 * t + i
                below = rolled(tile, 6 - 2 * i)
                extra = {5: 5, 7: 4, 8: 3}.get(field)
                if extra is not None:
                    below = jnp.where(sub == 5, rolled(last, extra), below)
                t2, i2 = divmod(field, 2)
                if field < 10:
                    above = from_above[pl.ds(x * 40 + 8 * t2, 8), :]
                    above = rolled(above, -3 * i2)
                else:
                    above = rolled(from_above[pl.ds(x * 40 + 8 * (field - 10), 8), :], 2)
                above = jnp.where(has_above, above, 0.0)
                rim[field, x] = jnp.where(sub < 4, above, below)
        return 0

    lax.fori_loop(0, nx, step, 0)
    for k, c in enumerate((0, 4, 3)):
        xsend[32 * k : 32 * k + nz, :] = fs[c, nx - 1]
        xsend[32 * k + nz : 32 * k + 32, :] = rim[3 + c, nx - 1]
    for k, c in enumerate((0, 3, 4)):
        xsend[96 + 8 * k : 104 + 8 * k, 0:128] = cs[c, cx - 1, 0:8]
        xsend[96 + 8 * k : 104 + 8 * k, 128:256] = cs[c, cx - 1, 8:16]
    xsend[120:128, :] = jnp.zeros((8, ny), F32)
    for k, c in enumerate((0, 3, 4)):
        at = nx * 40 + 8 + (3 + c) * cx + cx - 1
        xsend[120 + k : 121 + k, 0:128] = jnp.where(has_above[:, 0:128], from_above[at : at + 1, 0:128], 0.0)
    below = jnp.where(has_below[:, 0:128], from_below[nx * 32 + 16 :, 0:128], 0.0)
    above = jnp.where(has_above[:, 0:128], from_above[nx * 40 : nx * 40 + 8, 0:128], 0.0)
    turned = jnp.concatenate([raw[...], jnp.where(iota((RIM, 128), 0) < 4, above, below)], axis=0)
    for k in (1, 2):
        at = 96 + 32 * k
        xsend[at : at + nz, :] = fm[k, nx - 1]
        xsend[at + nz : at + 32, :] = rim[9 + k, nx - 1]
    xsend[192:208, 0:128] = turned[0:16]
    xsend[192:208, 128:256] = turned[16:32]
    for k, part in enumerate(fault_settings(turned)):
        settings[k] = part


def ring_back(a, _):
    return pltpu.roll(a, 1, 0)


def ring_fore(a, _):
    return pltpu.roll(a, a.shape[0] - 1, 0)


def reader(ref, rim, first):
    if ref.shape[1] == len(EDGES):
        return lambda c, x: ref[c, EDGES.index(x)]
    if ref.shape[2] == 32:
        return lambda c, x: ref[c, x]
    return lambda c, x: jnp.concatenate([ref[c, x], rim[first + c, x]], axis=0)


def held_column(bounds, cells, face, c, x):
    at = (face * 3 + c) * (bounds.shape[0] // 6) + x
    return jnp.sum(jnp.where(cells, bounds[at : at + 1, :], 0.0), axis=1, keepdims=True)


def held(value, columns):
    lane = iota(value.shape, 1)
    value = jnp.where(lane == 0, columns[0], value)
    return jnp.where(lane == value.shape[1] - 1, columns[1], value)


def merged(a):
    return jnp.where(iota((a.shape[0], 128), 1) < 64, a[:, 0:128], a[:, a.shape[1] - 128 :])


def velocity_planes(planes, v_ref, s_ref, m_ref, rim, behind, bounds_a, bounds_b, flags, put):
    bounds = bounds_a[...] + bounds_b[...]
    v, s, m = reader(v_ref, rim, 0), reader(s_ref, rim, 3), reader(m_ref, rim, 9)
    nz = 32
    cells = own_cells(flags, nz)
    has_x = has(flags, BEFORE_X)
    columns = {}
    for x in planes:
        here = [s(c, x) for c in FINE_S]
        if x // 3 not in columns:
            columns[x // 3] = [[held_column(bounds, cells, f, c, x // 3) for f in range(2)] for c in range(3)]
        if x == 0:
            before = [jnp.where(has_x, behind[k * nz : (k + 1) * nz, :], 0.0) for k in range(3)]
        else:
            before = [s(c, x - 1) for c in (0, 4, 3)]
        old = [v(c, x) for c in FINE_V]
        new = velocity_plane(old, here, before, (0.0,) * 3, m(0, x), ring_back)
        put(x, [held(new[k], columns[x // 3][c]) for k, c in enumerate(FINE_V)])


def velocity_edge_kernel(step, v, s, m, rim, behind, bounds_a, bounds_b, flags, *refs):
    refs = list(refs)
    more = [refs.pop(0)] if step == 1 else []
    nz = 32 if step < 2 else 24

    def put(x, new):
        for k in range(3):
            refs[0 if x == 0 else 1][k * nz : (k + 1) * nz, :] = new[k][0:nz]

    planes = [0] if step == 2 else [0, v.shape[1] - 1]
    velocity_planes(planes, v, s, m, rim, behind, bounds_a, bounds_b, flags, put)
    if step == 1:
        refs[0][3 * nz :, :] = more[0][...]


def fine_velocity_kernel(v, s, m, rim, behind, bounds_a, bounds_b, flags, out):
    def put(x, new):
        for k, c in enumerate(FINE_V):
            out[c, x] = new[k]

    velocity_planes(range(v.shape[1]), v, s, m, rim, behind, bounds_a, bounds_b, flags, put)


def share_kernel(v, s, m, behind, bounds_a, bounds_b, flags, share):
    nx, nz, ny = v.shape[1:]
    cx, own = nx // 3, nz - RIM
    bounds = bounds_a[...] + bounds_b[...]
    lane = iota((own, 128), 1)
    cells = own_cells(flags, own)

    def l_back(a):
        return pltpu.roll(a, 1, 1)

    columns = [[[held_column(bounds, cells, f, c, x) for f in range(2)] for c in range(3)] for x in range(cx)]
    sums = {}
    before = [merged(behind[k * nz : k * nz + own, :]) for k in range(3)]
    for x in range(nx):
        here = [merged(s[c, x]) for c in FINE_S]
        old = [merged(v[c, x, 0:own, :]) for c in FINE_V]
        rows = [here[k][nz - 1 : nz] for k in (3, 1, 5)]
        here = [a[0:own] for a in here]
        new = velocity_plane(old, here, before, rows, merged(m[0, x]), b_behind, l_back)
        before = [here[0], here[3], here[4]]
        for k, c in enumerate(FINE_V):
            val = held(new[k], columns[x // 3][c])
            sums[c, x // 3] = val if x % 3 == 0 else sums[c, x // 3] + val
    for f in range(2):
        face = lane < 3 if f == 0 else lane >= 125
        for c in range(3):
            for x in range(cx):
                at = (f * 3 + c) * cx + x
                total = jnp.sum(jnp.where(face, sums[c, x], 0.0), axis=1, keepdims=True)
                row = jnp.sum(jnp.where(cells, total, 0.0), axis=0, keepdims=True)
                share[at : at + 1, :] = row * (1.0 / 27.0)


def stress_planes(planes, s_ref, v_ref, m_ref, rim, xr, flags, put):
    v, s, m = reader(v_ref, rim, 0), reader(s_ref, rim, 3), reader(m_ref, rim, 9)
    nx, nz, half = s_ref.shape[1], 32, s_ref.shape[3] // 2
    has_x = has(flags, AFTER_X)
    lane = iota((nz, 128), 1)
    shear_plane = jnp.zeros((nz, 128), F32)
    for x in planes:
        here = [v(c, x) for c in FINE_V]
        if x == nx - 1:
            rows = nz if xr.shape[0] >= 3 * nz else nz - RIM
            after = [jnp.where(has_x, xr[k * rows : (k + 1) * rows, :], 0.0) for k in range(3)]
            if rows < nz:
                rest = jnp.zeros((nz - rows, xr.shape[1]), F32)
                after = [jnp.concatenate([plane, rest], axis=0) for plane in after]
        else:
            after = [v(c, x + 1) for c in FINE_V]
        old = [s(c, x) for c in FINE_S]
        new = stress_plane(old, here, after, (0.0,) * 3, m(1, x), m(2, x), ring_fore)
        put(x, new)
        moved = new[4][:, half : half + 128]
        moved = moved if x == 0 else pltpu.roll(moved, x, 1)
        shear_plane = jnp.where(lane == x, moved, shear_plane)
    return shear_plane


def friction(shear_plane, settings, old):
    traction = shear_plane + settings[1]
    weakened = jnp.minimum(old * settings[6], 1.0)
    strength = settings[2] * (settings[4] - settings[5] * weakened)
    resisted = jnp.clip(traction, -strength, strength)
    active = settings[3]
    fresh = old + active * STEP_RATIO * jnp.abs(traction - resisted)
    return fresh, shear_plane + active * (resisted - traction)


def with_fault(upper, fixed, x):
    moved = fixed if x == 0 else pltpu.roll(fixed, 128 - x, 1)
    return jnp.where(iota(upper.shape, 1) == 0, moved, upper)


def stress_behind(old, v_behind, v_first, given, slip, flags, out, slip_out):
    nz, half = 32, v_behind.shape[1] // 2
    has_x = has(flags, BEFORE_X)
    here = [v_behind[k * nz : (k + 1) * nz, :] for k in range(3)]
    xx, xb, xl = (old[k * nz : (k + 1) * nz, :] for k in range(3))
    lame, shear = given[128:160, :], given[160:192, :]
    new = stress_plane((xx, xx, xx, xb, xl, xl), here, v_first, (0.0,) * 3, lame, shear, ring_fore)
    turned = jnp.concatenate([given[192:208, 0:128], given[192:208, 128:256]], axis=0)
    settings = fault_settings(turned)
    last = 11
    xl = new[4]
    before = settings[0] if slip is None else slip[...]
    fresh, fixed = friction(pltpu.roll(xl[:, half : half + 128], last, 1), settings, before)
    if slip_out is not None:
        slip_out[...] = fresh
    xl = jnp.concatenate([xl[:, 0:half], with_fault(xl[:, half:], fixed, last)], axis=1)
    for k, value in enumerate((new[0], new[3], xl)):
        out[k * nz : (k + 1) * nz, :] = jnp.where(has_x, value, 0.0)


def stress_edge_kernel(s, v, m, rim, xr, settings, slip, flags, v_behind, given, out, behind, slip_behind):
    half = s.shape[3] // 2
    stress_behind(given, v_behind, [v[c, 0] for c in FINE_V], given, None, flags, behind, slip_behind)

    def put(x, new):
        for k, c in enumerate(FINE_S):
            out[c, EDGES.index(x)] = new[k]

    shear_plane = stress_planes(EDGES, s, v, m, rim, xr, flags, put)
    _, fixed = friction(shear_plane, settings, slip[...])
    for at, x in enumerate(EDGES):
        out[3, at, :, half:] = with_fault(out[3, at, :, half:], fixed, x)


def fine_stress_kernel(step, s, v, m, rim, xr, settings, slip, flags, *refs):
    last = step == 2
    copies = []
    nx, nz, half = s.shape[1], 32, s.shape[3] // 2
    own = nz - RIM
    if last:
        final, v_final, slip_final, mark, out, slip_out, sem = refs
        mark[...] = jnp.zeros_like(mark)
        copies.append(pltpu.make_async_copy(v.at[:, :, 0:own, :], v_final, sem.at[0]))
        copies[0].start()
    else:
        if step == 1:
            v_behind, given, old, slip_before, out, slip_out, behind = refs
            first = [v[c, 0] for c in FINE_V]
            stress_behind(old, v_behind, first, given, slip_before, flags, behind, None)
        else:
            out, slip_out = refs

    def put(x, new):
        for k, c in enumerate(FINE_S):
            out[c, x] = new[k]
        if last:
            for first, end in ((0, 3), (4, 6)):
                at = len(copies)
                copies.append(
                    pltpu.make_async_copy(out.at[first:end, x, 0:own, :], final.at[first:end, x], sem.at[at])
                )
                copies[at].start()

    shear_plane = stress_planes(range(nx), s, v, m, rim, xr, flags, put)
    fresh, fixed = friction(shear_plane, settings, slip[...])
    for x in range(nx):
        out[3, x, :, half:] = with_fault(out[3, x, :, half:], fixed, x)
    if last:
        copies.append(pltpu.make_async_copy(out.at[3, :, 0:own, :], final.at[3], sem.at[len(copies)]))
        copies[-1].start()
        turned = jnp.concatenate([fresh, jnp.zeros((128 - nz, 128), F32)], axis=0).T
        slip_out[...] = turned[0:nx, 0:own]
        copies.append(pltpu.make_async_copy(slip_out, slip_final, sem.at[len(copies)]))
        copies[-1].start()
        for copy in copies:
            copy.wait()
    else:
        slip_out[...] = fresh


def coarse_velocity_kernel(cv, cs, cm, xr, below, above, rows_ref, flags, out, xsend, next_rows, cs_near, cm_near):
    nx, ny, nz = cv.shape[1:]
    has_x, has_y = has(flags, BEFORE_X)[:, 0:128], has(flags, BEFORE_Z)[:, 0:128]
    more = has(flags, AFTER_Z)[:, 0:128]
    low, high = below.shape[0] - 24, above.shape[0] - 40
    cs_near[...] = cs[...]
    cm_near[...] = cm[...]
    xsend[...] = jnp.zeros_like(xsend)
    next_rows[3 * nx :, :] = jnp.zeros_like(next_rows[3 * nx :, :])

    def ahead(field, x):
        at = high + field * nx + x
        return jnp.where(more, above[at : at + 1, 0:128], 0.0)

    for x in range(nx):
        here = [cs[c, x] for c in COARSE_S]
        here_row = [ahead(3 + c, x) for c in COARSE_S]
        if x == 0:
            before, before_row = [], []
            for k in range(3):
                at = 96 + 8 * k
                plane = jnp.concatenate([xr[at : at + 8, 0:128], xr[at : at + 8, 128:256]], axis=0)
                before.append(jnp.where(has_x, plane, 0.0))
                before_row.append(jnp.where(has_x, xr[120 + k : 121 + k, 0:128], 0.0))
        else:
            before = [cs[c, x - 1] for c in (0, 3, 4)]
            before_row = [ahead(3 + c, x - 1) for c in (0, 3, 4)]
        rows = [jnp.where(has_y, below[low + k * nx + x : low + k * nx + x + 1, 0:128], 0.0) for k in range(3)]
        new = velocity_plane([cv[c, x] for c in COARSE_V], here, before, rows, cm[0, x])
        last = [here[k][ny - 1 : ny] for k in (3, 1, 5)]
        old_row = [ahead(c, x) for c in COARSE_V]
        new_row = velocity_plane(old_row, here_row, before_row, last, ahead(9, x), lambda a, edge: edge)
        for c in range(3):
            out[c, x] = new[c]
            next_rows[c * nx + x : c * nx + x + 1, :] = new_row[c]
            if x == 0:
                xsend[8 * c : 8 * c + 8, 0:128] = new[c][0:8]
                xsend[8 * c : 8 * c + 8, 128:256] = new[c][8:16]
    for f in range(2):
        xsend[24 + f : 25 + f, 0:128] = rows_ref[f, 0:1, :].astype(F32)


def coarse_stress_kernel(cv, cs, cm, xr, zr, rows_ref, rest, rest_next, flags, _, v_out, s_out):
    nx, ny, nz = cv.shape[1:]
    base = xr.shape[0] - 32
    has_x, has_y = has(flags, AFTER_X)[:, 0:128], has(flags, AFTER_Z)[:, 0:128]
    row_ids = own_rows(flags, (ny, nz))

    def inserted(plane, c, x):
        for f in range(2):
            if x < nx:
                hit = row_ids == rows_ref[f, x : x + 1, :].astype(F32)
            else:
                hit = row_ids == xr[base + 24 + f : base + 25 + f, 0:128]
            at = (f * 3 + c) * nx + x % nx
            value = rest[at : at + 1, :] if x < nx else rest_next[at : at + 1, :]
            plane = jnp.where(hit, value, plane)
        return plane

    planes = [[inserted(cv[c, x], c, x) for c in range(3)] for x in range(nx)]
    edge = []
    for c in range(3):
        at = base + 8 * c
        plane = jnp.concatenate([xr[at : at + 8, 0:128], xr[at : at + 8, 128:256]], axis=0)
        edge.append(jnp.where(has_x, inserted(plane, c, nx), 0.0))
    planes.append(edge)
    for x in range(nx):
        for c in range(3):
            v_out[c, x] = planes[x][c]
        rows = [jnp.where(has_y, zr[k * nx + x : k * nx + x + 1, :], 0.0) for k in range(3)]
        new = stress_plane([cs[c, x] for c in COARSE_S], planes[x], planes[x + 1], rows, cm[1, x], cm[2, x])
        for c in range(6):
            s_out[c, x] = new[c]


def swap(value, axis, bit):
    count = lax.axis_size(axis)
    return lax.ppermute(value, axis, [(i, i ^ bit) for i in range(count)])


def apart(value, out):
    parts = []
    for turn in range(1, 8):
        pairs = [(home, 2 * ((home // 2 + turn) % 8) + home % 2) for home in (5, 10)]
        parts.append(lax.ppermute(value, "gy", [pair if out else pair[::-1] for pair in pairs]))
    return parts


def body(
    coarse_velocity,
    coarse_stress,
    coarse_material,
    fine_velocity,
    fine_stress,
    fine_material,
    fault_slip,
    initial_shear,
    normal_stress,
    fault_mask,
    zone_ids,
    static_friction,
    friction_drop,
    weakening_distance,
    owner_rows,
):
    nx, nz, ny = fine_velocity.shape[1:]
    cx, cy, cz = coarse_velocity.shape[1:]
    flags = make_flags(nz // 3, cy)
    shares = (6 * cx, cz)
    fault = (fault_slip, initial_shear, normal_stress, fault_mask, zone_ids)
    fields = (fine_velocity, fine_stress, fine_material)
    zoned = (static_friction, friction_drop, weakening_distance)
    given = [
        pltpu.with_memory_space_constraint(a, pltpu.HBM)
        for a in fields + (coarse_stress, coarse_velocity, coarse_material) + fault + zoned + (owner_rows,)
    ]
    up, down, raw = pl.pallas_call(
        pack_kernel,
        out_shape=[
            jax.ShapeDtypeStruct(shape, F32) for shape in ((nx * 32 + 24, ny), (nx * 40 + 48, ny), (nz, 128))
        ],
        in_specs=[HBM] * 14 + [VMEM],
        out_specs=[VMEM] * 3,
        scratch_shapes=[pltpu.VMEM((a.shape[0], nx, 8, ny), F32) for a in fields * 2]
        + [pltpu.VMEM((c, cx, 8, cz), F32) for c in (3, 3, 6)]
        + [pltpu.VMEM((cx, 8, cz), F32)]
        + [pltpu.SMEM(a.shape, F32) for a in zoned]
        + [pltpu.VMEM(a.shape, a.dtype) for a in fault]
        + [pltpu.VMEM((128, 128), F32), pltpu.SemaphoreType.DMA((20,))],
        compiler_params=PARAMS,
    )(*given[:14], flags)
    coupling = pl.pallas_call(
        coupling_kernel,
        out_shape=jax.ShapeDtypeStruct(shares, F32),
        in_specs=[HBM] * 2 + [VMEM] * 2,
        out_specs=VMEM,
        scratch_shapes=[
            pltpu.VMEM(coarse_velocity.shape, F32),
            pltpu.VMEM(owner_rows.shape, jnp.int32),
            pltpu.SemaphoreType.DMA((2,)),
        ],
        compiler_params=PARAMS,
    )(given[4], given[14], flags, raw)
    from_below, from_above = ring(up, "gy", 1), ring(down, "gy", -1)
    parts = apart(coupling, True)
    rim, xsend, settings = call(
        rim_kernel,
        [(12, nx, RIM, ny), (208, ny), (7, 32, 128)],
        [VMEM] * 7,
        from_below, from_above, fine_stress, fine_material, coarse_stress, raw, flags,
    )
    slip = settings[0]
    xr = ring(xsend, "gx", 1)
    bounds = coupling + sum(parts[1:], parts[0])
    bounds = (bounds, swap(bounds, "gy", 1))
    coarse_moved, cxs, coarse_zr, coarse_stress, coarse_material = call(
        coarse_velocity_kernel,
        [coarse_velocity.shape, (32, ny), (16, cz), coarse_stress.shape, coarse_material.shape],
        [VMEM] * 8,
        coarse_velocity, coarse_stress, coarse_material, xr, from_below, from_above, owner_rows, flags,
    )
    velocity, stress = fine_velocity, fine_stress

    def velocity_half(step, behind, *to_send):
        args = (velocity, stress, fine_material, rim, behind, *bounds, flags)
        near = (velocity, edges, *args[2:]) if step == 1 else args
        sends = call(
            lambda *refs: velocity_edge_kernel(step, *refs),
            [(96, ny), (96, ny)] if step == 0 else [(128, ny), (96, ny)] if step == 1 else [(72, ny)],
            [VMEM] * (8 + len(to_send) * (step < 2)), *near, *(to_send if step < 2 else ()),
        )
        sends = list(sends)
        if step == 2:
            sends[0], *to_send = lax.optimization_barrier((sends[0], *to_send))
        moved = [ring(send, "gx", way) for send, way in zip(sends, (-1, 1))]
        (new,) = call(fine_velocity_kernel, [(3, nx, 32, ny)], [VMEM] * 8, *args)
        return (new, moved, *to_send) if step == 2 else (new, moved)

    def stress_half(step, xr, *more):
        return call(
            lambda *refs: fine_stress_kernel(step, *refs),
            [(6, nx, 32, ny), (32, 128), (96, ny)][: 2 + step], [VMEM] * (8 + len(more)),
            stress, velocity, fine_material, rim, xr, settings, slip, flags, *more,
        )

    given_behind = xr
    velocity, (xr, v_behind) = velocity_half(0, given_behind)
    edges, behind, slip_behind = call(
        stress_edge_kernel, [(6, len(EDGES), 32, ny), (96, ny), (32, 128)], [VMEM] * 10,
        stress, velocity, fine_material, rim, xr, settings, slip, flags, v_behind, given_behind,
    )
    stress, slip = stress_half(0, xr)
    velocity, (coarse_xr, v_behind) = velocity_half(1, behind, cxs)
    stress, slip, behind = stress_half(1, coarse_xr, v_behind, given_behind, behind, slip_behind)
    (share,) = call(share_kernel, [shares], [VMEM] * 7, velocity, stress, fine_material, behind, *bounds, flags)
    share = share + swap(share, "gy", 1)
    velocity, (xr,), share = velocity_half(2, behind, share)
    parts = apart(share, False)
    restricted = share + sum(parts[1:], parts[0])
    restricted_next = ring(restricted, "gx", -1)
    stress, velocity, slip, mark = pl.pallas_call(
        lambda *refs: fine_stress_kernel(2, *refs),
        out_shape=[jax.ShapeDtypeStruct(a.shape, F32) for a in (fine_stress, fine_velocity, fault_slip, raw[0:8])],
        in_specs=[VMEM] * 8,
        out_specs=[pl.BlockSpec(memory_space=pl.ANY)] * 3 + [VMEM],
        scratch_shapes=[
            pltpu.VMEM((6, nx, 32, ny), F32),
            pltpu.VMEM(fault_slip.shape, F32),
            pltpu.SemaphoreType.DMA((2 * nx + 3,)),
        ],
        compiler_params=PARAMS,
    )(stress, velocity, fine_material, rim, xr, settings, slip, flags)
    coarse_next, coarse_stress_next = call(
        coarse_stress_kernel,
        [coarse_velocity.shape, coarse_stress.shape],
        [VMEM] * 10,
        coarse_moved, coarse_stress, coarse_material, coarse_xr, coarse_zr, owner_rows, restricted, restricted_next,
        flags, mark,
    )
    return (coarse_next, coarse_stress_next, velocity, stress, slip)


def solution(mesh):
    grid = P(None, "gx", "gy", None)
    plane = P("gx", "gy")
    return jax.shard_map(
        body,
        mesh=mesh,
        in_specs=(grid,) * 6 + (plane,) * 5 + (P(),) * 3 + (P(None, "gx", None),),
        out_specs=(grid,) * 4 + (plane,),
        check_vma=False,
    )
```

```python
import jax
import jax.numpy as jnp
from jax import lax
from jax.experimental import pallas as pl
from jax.experimental.pallas import tpu as pltpu
from jax.sharding import PartitionSpec as P

STEP_RATIO = 0.15
F32 = jnp.float32
FINE_S = (0, 2, 1, 4, 3, 5)
FINE_V = (0, 2, 1)
COARSE_S = (0, 1, 2, 3, 4, 5)
COARSE_V = (0, 1, 2)
VMEM = pl.BlockSpec(memory_space=pltpu.VMEM)
SMEM = pl.BlockSpec(memory_space=pltpu.SMEM)
HBM = pl.BlockSpec(memory_space=pltpu.HBM)
PARAMS = pltpu.CompilerParams(vmem_limit_bytes=8 * 1024 * 1024)


def call(kernel, outs, specs, *args):
    return pl.pallas_call(
        kernel,
        out_shape=tuple(jax.ShapeDtypeStruct(shape, F32) for shape in outs),
        in_specs=list(specs),
        out_specs=tuple(VMEM for _ in outs),
        compiler_params=PARAMS,
    )(*args)


def ring(value, axis, steps):
    count = lax.axis_size(axis)
    return lax.ppermute(value, axis, [(i, (i + steps) % count) for i in range(count)])


def iota(shape, along):
    return lax.broadcasted_iota(jnp.int32, shape, along)


def b_behind(a, edge):
    return jnp.where(iota(a.shape, 0) == 0, edge, pltpu.roll(a, 1, 0))


def b_ahead(a, edge):
    last = a.shape[0] - 1
    return jnp.where(iota(a.shape, 0) == last, edge, pltpu.roll(a, last, 0))


def l_behind(a):
    return jnp.where(iota(a.shape, 1) == 0, 0.0, pltpu.roll(a, 1, 1))


def l_ahead(a):
    last = a.shape[1] - 1
    return jnp.where(iota(a.shape, 1) == last, 0.0, pltpu.roll(a, last, 1))


def velocity_plane(v, s, s_prev, rows, buoyancy, b_back=b_behind, l_back=l_behind):
    xx, bb, ll, xb, xl, bl = s
    p_xx, p_xb, p_xl = s_prev
    r_xb, r_bb, r_bl = rows
    f_x = (xx - p_xx) + (xb - b_back(xb, r_xb)) + (xl - l_back(xl))
    f_b = (xb - p_xb) + (bb - b_back(bb, r_bb)) + (bl - l_back(bl))
    f_l = (xl - p_xl) + (bl - b_back(bl, r_bl)) + (ll - l_back(ll))
    scale = STEP_RATIO * buoyancy
    return (v[0] + scale * f_x, v[1] + scale * f_b, v[2] + scale * f_l)


def stress_plane(s, v, v_next, rows, lame, shear, b_fore=b_ahead, l_fore=l_ahead):
    vx, vb, vl = v
    nx, nb, nl = v_next
    rx, rb, rl = rows
    e_x = nx - vx
    e_b = b_fore(vb, rb) - vb
    e_l = l_fore(vl) - vl
    e_xb = (b_fore(vx, rx) - vx) + (nb - vb)
    e_xl = (l_fore(vx) - vx) + (nl - vl)
    e_bl = (b_fore(vl, rl) - vl) + (l_fore(vb) - vb)
    common = (STEP_RATIO * lame) * (e_x + e_b + e_l)
    one = STEP_RATIO * shear
    two = 2.0 * one
    return (
        s[0] + (common + two * e_x),
        s[1] + (common + two * e_b),
        s[2] + (common + two * e_l),
        s[3] + one * e_xb,
        s[4] + one * e_xl,
        s[5] + one * e_bl,
    )


BEFORE_X, AFTER_X, BEFORE_Z, AFTER_Z, FIRST_CELL, FIRST_ROW = range(6)


def make_flags(cells, rows):
    gx, gy = lax.axis_index("gx"), lax.axis_index("gy")
    last_x, last_y = lax.axis_size("gx") - 1, lax.axis_size("gy") - 1
    values = (gx > 0, gx < last_x, gy > 0, gy < last_y, gy * cells, gy * rows, gx, gy)
    values = jnp.stack([jnp.asarray(v).astype(F32) for v in values])
    return jnp.broadcast_to(values[:, None], (8, 256))


def has(flags, which):
    return flags[which : which + 1, :] > 0.5


def own_cells(flags, depth):
    shape = (depth, 128)
    row = iota(shape, 0)
    cell = iota(shape, 1) - jnp.where(row < 27, row // 3, -1)
    return cell.astype(F32) == flags[FIRST_CELL : FIRST_CELL + 1, 0:128]


def own_rows(flags, shape):
    return iota(shape, 0).astype(F32) + flags[FIRST_ROW : FIRST_ROW + 1, 0:128]


RIM = 8
EDGES = (0, 10, 11)


def part_of(field, refs):
    if field < 3:
        return refs[0], field
    if field < 9:
        return refs[1], field - 3
    return refs[2], field - 9


def coupling_kernel(cv, rows_hbm, flags, _, coupling, cv_buf, rows_ref, sem):
    cx, cy, cz = cv.shape[1:]
    moves = ((cv, cv_buf), (rows_hbm, rows_ref))
    copies = [pltpu.make_async_copy(src, dst, sem.at[i]) for i, (src, dst) in enumerate(moves)]
    for copy in copies:
        copy.start()
    for copy in copies:
        copy.wait()
    ids = own_rows(flags, (cy, cz))
    for f in range(2):
        for x in range(cx):
            here = ids == rows_ref[f, x : x + 1, :].astype(F32)
            for c in range(3):
                row = jnp.sum(jnp.where(here, cv_buf[c, x], 0.0), axis=0, keepdims=True)
                at = (f * 3 + c) * cx + x
                coupling[at : at + 1, :] = row


def pack_kernel(
    fv, fs, fm, cs, cv, cm, slip, shear, normal, mask, zone, static, drop, distance, _,
    up, down, raw,
    top_v, top_s, top_m, low_v, low_s, low_m, cz_buf, cv_low, cs_low, cm_low, static_buf, drop_buf, distance_buf, slip_buf, shear_buf, normal_buf, mask_buf, zone_buf, turn, sem,
):
    nx, nz, ny = fv.shape[1:]
    cx, cy, cz = cs.shape[1:]
    fault = (slip_buf, shear_buf, normal_buf, mask_buf, zone_buf)
    zoned = (static_buf, drop_buf, distance_buf)
    moves = list(zip((slip, shear, normal, mask, zone, static, drop, distance), fault + zoned))
    moves.append((cv.at[:, :, 0:8, :], cv_low))
    for k, c in enumerate((3, 1, 5)):
        moves.append((cs.at[c, :, cy - 8 : cy, :], cz_buf.at[k]))
    moves.append((cs.at[:, :, 0:8, :], cs_low))
    moves.append((cm.at[0, :, 0:8, :], cm_low))
    early = len(moves)
    for src, top, low in ((fv, top_v, low_v), (fs, top_s, low_s), (fm, top_m, low_m)):
        moves.append((src.at[:, :, nz - 8 : nz, :], top))
        moves.append((src.at[:, :, 0:8, :], low))
    copies = [pltpu.make_async_copy(src, dst, sem.at[i]) for i, (src, dst) in enumerate(moves)]
    for copy in copies:
        copy.start()
    for copy in copies[:early]:
        copy.wait()
    turn[...] = jnp.zeros_like(turn)
    for k, ref in enumerate(fault):
        turn[16 * k : 16 * k + nx, 0:nz] = ref[...].astype(F32)
    turned = turn[...].T[0:nz]
    zones = pltpu.roll(turned, 128 - 64, 1)
    group = iota(turned.shape, 1) // 16
    for k in range(3):
        value = jnp.zeros_like(turned)
        for zone_id in range(4):
            part = zoned[k][zone_id]
            if k == 2:
                part = 1.0 / jnp.full(turned.shape, part)
            value = jnp.where(zones == float(zone_id), part, value)
        turned = jnp.where(group == 5 + k, pltpu.roll(value, 16 * (5 + k), 1), turned)
    raw[...] = turned
    at = nx * 32
    up[at:, :] = jnp.zeros((24, ny), F32)
    for k in range(3):
        for x in range(cx):
            up[at + k * cx + x : at + k * cx + x + 1, 0:128] = cz_buf[k, x, 7:8]
    up[at + 16 : at + 24, 0:128] = turned[nz - 8 :]
    down[nx * 40 :, :] = jnp.zeros((48, ny), F32)
    down[nx * 40 : nx * 40 + 8, 0:128] = turned[0:8]
    for c in range(10):
        for x in range(cx):
            if c < 3:
                row = cv_low[c, x, 0:1]
            elif c < 9:
                row = cs_low[c - 3, x, 0:1]
            else:
                row = cm_low[x, 0:1]
            at = nx * 40 + 8 + c * cx + x
            down[at : at + 1, 0:128] = row
    for copy in copies[early:]:
        copy.wait()
    tops, lows = (top_v, top_s, top_m), (low_v, low_s, low_m)
    sub = iota((RIM, ny), 0)

    def rolled(tile, by):
        return pltpu.roll(tile, by % RIM, 0) if by % RIM else tile

    def step(x, _):
        def take(refs, field):
            ref, c = part_of(field, refs)
            return ref[c, x]

        for t in range(3):
            tile = rolled(take(tops, 4 * t), -6)
            for i in range(1, 4):
                tile = jnp.where(sub // 2 == i, rolled(take(tops, 4 * t + i), 2 * i - 6), tile)
            up[pl.ds(x * 32 + 8 * t, 8), :] = tile
        tile = rolled(take(tops, 3 + 2), -5)
        tile = jnp.where(sub == 1, rolled(take(tops, 3 + 4), -4), tile)
        tile = jnp.where(sub == 2, rolled(take(tops, 3 + 5), -3), tile)
        up[pl.ds(x * 32 + 24, 8), :] = tile
        for t in range(5):
            tile = jnp.where(sub < 3, take(lows, 2 * t), rolled(take(lows, 2 * t + 1), 3))
            if t < 2:
                tile = jnp.where(sub < 6, tile, rolled(take(lows, 10 + t), 6))
            down[pl.ds(x * 40 + 8 * t, 8), :] = tile
        return 0

    lax.fori_loop(0, nx, step, 0)


def add_up(parts):
    total = parts[0][...]
    for part in parts[1:]:
        total = total + part[...]
    return total


def fault_settings(turned):
    return [turned] + [pltpu.roll(turned, 128 - 16 * k, 1) for k in (1, 2, 3, 5, 6, 7)]


def rim_kernel(from_below, from_above, fs, fm, cs, raw, flags, rim, xsend, settings):
    nx, nz, ny = fs.shape[1:]
    cx = cs.shape[1]
    has_below, has_above = has(flags, BEFORE_Z), has(flags, AFTER_Z)
    sub = iota((RIM, ny), 0)

    def rolled(tile, by):
        return pltpu.roll(tile, by % RIM, 0) if by % RIM else tile

    def step(x, _):
        last = jnp.where(has_below, from_below[pl.ds(x * 32 + 24, 8), :], 0.0)
        for t in range(3):
            tile = jnp.where(has_below, from_below[pl.ds(x * 32 + 8 * t, 8), :], 0.0)
            for i in range(4):
                field = 4 * t + i
                below = rolled(tile, 6 - 2 * i)
                extra = {5: 5, 7: 4, 8: 3}.get(field)
                if extra is not None:
                    below = jnp.where(sub == 5, rolled(last, extra), below)
                t2, i2 = divmod(field, 2)
                if field < 10:
                    above = from_above[pl.ds(x * 40 + 8 * t2, 8), :]
                    above = rolled(above, -3 * i2)
                else:
                    above = rolled(from_above[pl.ds(x * 40 + 8 * (field - 10), 8), :], 2)
                above = jnp.where(has_above, above, 0.0)
                rim[field, x] = jnp.where(sub < 4, above, below)
        return 0

    lax.fori_loop(0, nx, step, 0)
    for k, c in enumerate((0, 4, 3)):
        xsend[32 * k : 32 * k + nz, :] = fs[c, nx - 1]
        xsend[32 * k + nz : 32 * k + 32, :] = rim[3 + c, nx - 1]
    for k, c in enumerate((0, 3, 4)):
        xsend[96 + 8 * k : 104 + 8 * k, 0:128] = cs[c, cx - 1, 0:8]
        xsend[96 + 8 * k : 104 + 8 * k, 128:256] = cs[c, cx - 1, 8:16]
    xsend[120:128, :] = jnp.zeros((8, ny), F32)
    for k, c in enumerate((0, 3, 4)):
        at = nx * 40 + 8 + (3 + c) * cx + cx - 1
        xsend[120 + k : 121 + k, 0:128] = jnp.where(has_above[:, 0:128], from_above[at : at + 1, 0:128], 0.0)
    below = jnp.where(has_below[:, 0:128], from_below[nx * 32 + 16 :, 0:128], 0.0)
    above = jnp.where(has_above[:, 0:128], from_above[nx * 40 : nx * 40 + 8, 0:128], 0.0)
    turned = jnp.concatenate([raw[...], jnp.where(iota((RIM, 128), 0) < 4, above, below)], axis=0)
    for k in (1, 2):
        at = 96 + 32 * k
        xsend[at : at + nz, :] = fm[k, nx - 1]
        xsend[at + nz : at + 32, :] = rim[9 + k, nx - 1]
    xsend[192:208, 0:128] = turned[0:16]
    xsend[192:208, 128:256] = turned[16:32]
    for k, part in enumerate(fault_settings(turned)):
        settings[k] = part


def ring_back(a, _):
    return pltpu.roll(a, 1, 0)


def ring_fore(a, _):
    return pltpu.roll(a, a.shape[0] - 1, 0)


def reader(ref, rim, first):
    if ref.shape[1] == len(EDGES):
        return lambda c, x: ref[c, EDGES.index(x)]
    if ref.shape[2] == 32:
        return lambda c, x: ref[c, x]
    return lambda c, x: jnp.concatenate([ref[c, x], rim[first + c, x]], axis=0)


def held_column(bounds, cells, face, c, x):
    at = (face * 3 + c) * (bounds.shape[0] // 6) + x
    return jnp.sum(jnp.where(cells, bounds[at : at + 1, :], 0.0), axis=1, keepdims=True)


def held(value, columns):
    lane = iota(value.shape, 1)
    value = jnp.where(lane == 0, columns[0], value)
    return jnp.where(lane == value.shape[1] - 1, columns[1], value)


def merged(a):
    return jnp.where(iota((a.shape[0], 128), 1) < 64, a[:, 0:128], a[:, a.shape[1] - 128 :])


def velocity_planes(planes, v_ref, s_ref, m_ref, rim, behind, bounds_a, bounds_b, flags, put):
    bounds = bounds_a[...] + bounds_b[...]
    v, s, m = reader(v_ref, rim, 0), reader(s_ref, rim, 3), reader(m_ref, rim, 9)
    nz = 32
    cells = own_cells(flags, nz)
    has_x = has(flags, BEFORE_X)
    columns = {}
    for x in planes:
        here = [s(c, x) for c in FINE_S]
        if x // 3 not in columns:
            columns[x // 3] = [[held_column(bounds, cells, f, c, x // 3) for f in range(2)] for c in range(3)]
        if x == 0:
            before = [jnp.where(has_x, behind[k * nz : (k + 1) * nz, :], 0.0) for k in range(3)]
        else:
            before = [s(c, x - 1) for c in (0, 4, 3)]
        old = [v(c, x) for c in FINE_V]
        new = velocity_plane(old, here, before, (0.0,) * 3, m(0, x), ring_back)
        put(x, [held(new[k], columns[x // 3][c]) for k, c in enumerate(FINE_V)])


def velocity_edge_kernel(step, v, s, m, rim, behind, bounds_a, bounds_b, flags, *refs):
    refs = list(refs)
    more = [refs.pop(0)] if step == 1 else []
    nz = 32 if step < 2 else 24

    def put(x, new):
        for k in range(3):
            refs[0 if x == 0 else 1][k * nz : (k + 1) * nz, :] = new[k][0:nz]

    planes = [0] if step == 2 else [0, v.shape[1] - 1]
    velocity_planes(planes, v, s, m, rim, behind, bounds_a, bounds_b, flags, put)
    if step == 1:
        refs[0][3 * nz :, :] = more[0][...]


def fine_velocity_kernel(v, s, m, rim, behind, bounds_a, bounds_b, flags, out):
    def put(x, new):
        for k, c in enumerate(FINE_V):
            out[c, x] = new[k]

    velocity_planes(range(v.shape[1]), v, s, m, rim, behind, bounds_a, bounds_b, flags, put)


def share_kernel(v, s, m, behind, bounds_a, bounds_b, flags, share):
    nx, nz, ny = v.shape[1:]
    cx, own = nx // 3, nz - RIM
    bounds = bounds_a[...] + bounds_b[...]
    lane = iota((own, 128), 1)
    cells = own_cells(flags, own)

    def l_back(a):
        return pltpu.roll(a, 1, 1)

    columns = [[[held_column(bounds, cells, f, c, x) for f in range(2)] for c in range(3)] for x in range(cx)]
    sums = {}
    before = [merged(behind[k * nz : k * nz + own, :]) for k in range(3)]
    for x in range(nx):
        here = [merged(s[c, x]) for c in FINE_S]
        old = [merged(v[c, x, 0:own, :]) for c in FINE_V]
        rows = [here[k][nz - 1 : nz] for k in (3, 1, 5)]
        here = [a[0:own] for a in here]
        new = velocity_plane(old, here, before, rows, merged(m[0, x]), b_behind, l_back)
        before = [here[0], here[3], here[4]]
        for k, c in enumerate(FINE_V):
            val = held(new[k], columns[x // 3][c])
            sums[c, x // 3] = val if x % 3 == 0 else sums[c, x // 3] + val
    for f in range(2):
        face = lane < 3 if f == 0 else lane >= 125
        for c in range(3):
            for x in range(cx):
                at = (f * 3 + c) * cx + x
                total = jnp.sum(jnp.where(face, sums[c, x], 0.0), axis=1, keepdims=True)
                row = jnp.sum(jnp.where(cells, total, 0.0), axis=0, keepdims=True)
                share[at : at + 1, :] = row * (1.0 / 27.0)


def stress_planes(planes, s_ref, v_ref, m_ref, rim, xr, flags, put):
    v, s, m = reader(v_ref, rim, 0), reader(s_ref, rim, 3), reader(m_ref, rim, 9)
    nx, nz, half = s_ref.shape[1], 32, s_ref.shape[3] // 2
    has_x = has(flags, AFTER_X)
    lane = iota((nz, 128), 1)
    shear_plane = jnp.zeros((nz, 128), F32)
    for x in planes:
        here = [v(c, x) for c in FINE_V]
        if x == nx - 1:
            rows = nz if xr.shape[0] >= 3 * nz else nz - RIM
            after = [jnp.where(has_x, xr[k * rows : (k + 1) * rows, :], 0.0) for k in range(3)]
            if rows < nz:
                rest = jnp.zeros((nz - rows, xr.shape[1]), F32)
                after = [jnp.concatenate([plane, rest], axis=0) for plane in after]
        else:
            after = [v(c, x + 1) for c in FINE_V]
        old = [s(c, x) for c in FINE_S]
        new = stress_plane(old, here, after, (0.0,) * 3, m(1, x), m(2, x), ring_fore)
        put(x, new)
        moved = new[4][:, half : half + 128]
        moved = moved if x == 0 else pltpu.roll(moved, x, 1)
        shear_plane = jnp.where(lane == x, moved, shear_plane)
    return shear_plane


def friction(shear_plane, settings, old):
    traction = shear_plane + settings[1]
    weakened = jnp.minimum(old * settings[6], 1.0)
    strength = settings[2] * (settings[4] - settings[5] * weakened)
    resisted = jnp.clip(traction, -strength, strength)
    active = settings[3]
    fresh = old + active * STEP_RATIO * jnp.abs(traction - resisted)
    return fresh, shear_plane + active * (resisted - traction)


def with_fault(upper, fixed, x):
    moved = fixed if x == 0 else pltpu.roll(fixed, 128 - x, 1)
    return jnp.where(iota(upper.shape, 1) == 0, moved, upper)


def stress_behind(old, v_behind, v_first, given, slip, flags, out, slip_out):
    nz, half = 32, v_behind.shape[1] // 2
    has_x = has(flags, BEFORE_X)
    here = [v_behind[k * nz : (k + 1) * nz, :] for k in range(3)]
    xx, xb, xl = (old[k * nz : (k + 1) * nz, :] for k in range(3))
    lame, shear = given[128:160, :], given[160:192, :]
    new = stress_plane((xx, xx, xx, xb, xl, xl), here, v_first, (0.0,) * 3, lame, shear, ring_fore)
    turned = jnp.concatenate([given[192:208, 0:128], given[192:208, 128:256]], axis=0)
    settings = fault_settings(turned)
    last = 11
    xl = new[4]
    before = settings[0] if slip is None else slip[...]
    fresh, fixed = friction(pltpu.roll(xl[:, half : half + 128], last, 1), settings, before)
    if slip_out is not None:
        slip_out[...] = fresh
    xl = jnp.concatenate([xl[:, 0:half], with_fault(xl[:, half:], fixed, last)], axis=1)
    for k, value in enumerate((new[0], new[3], xl)):
        out[k * nz : (k + 1) * nz, :] = jnp.where(has_x, value, 0.0)


def stress_edge_kernel(s, v, m, rim, xr, settings, slip, flags, v_behind, given, out, behind, slip_behind):
    half = s.shape[3] // 2
    stress_behind(given, v_behind, [v[c, 0] for c in FINE_V], given, None, flags, behind, slip_behind)

    def put(x, new):
        for k, c in enumerate(FINE_S):
            out[c, EDGES.index(x)] = new[k]

    shear_plane = stress_planes(EDGES, s, v, m, rim, xr, flags, put)
    _, fixed = friction(shear_plane, settings, slip[...])
    for at, x in enumerate(EDGES):
        out[3, at, :, half:] = with_fault(out[3, at, :, half:], fixed, x)


def fine_stress_kernel(step, s, v, m, rim, xr, settings, slip, flags, *refs):
    last = step == 2
    copies = []
    nx, nz, half = s.shape[1], 32, s.shape[3] // 2
    own = nz - RIM
    if last:
        final, v_final, slip_final, mark, out, slip_out, sem = refs
        mark[...] = jnp.zeros_like(mark)
        copies.append(pltpu.make_async_copy(v.at[:, :, 0:own, :], v_final, sem.at[0]))
        copies[0].start()
    else:
        if step == 1:
            v_behind, given, old, slip_before, out, slip_out, behind = refs
            first = [v[c, 0] for c in FINE_V]
            stress_behind(old, v_behind, first, given, slip_before, flags, behind, None)
        else:
            out, slip_out = refs

    def put(x, new):
        for k, c in enumerate(FINE_S):
            out[c, x] = new[k]
        if last:
            for first, end in ((0, 3), (4, 6)):
                at = len(copies)
                copies.append(
                    pltpu.make_async_copy(out.at[first:end, x, 0:own, :], final.at[first:end, x], sem.at[at])
                )
                copies[at].start()

    shear_plane = stress_planes(range(nx), s, v, m, rim, xr, flags, put)
    fresh, fixed = friction(shear_plane, settings, slip[...])
    for x in range(nx):
        out[3, x, :, half:] = with_fault(out[3, x, :, half:], fixed, x)
    if last:
        copies.append(pltpu.make_async_copy(out.at[3, :, 0:own, :], final.at[3], sem.at[len(copies)]))
        copies[-1].start()
        turned = jnp.concatenate([fresh, jnp.zeros((128 - nz, 128), F32)], axis=0).T
        slip_out[...] = turned[0:nx, 0:own]
        copies.append(pltpu.make_async_copy(slip_out, slip_final, sem.at[len(copies)]))
        copies[-1].start()
        for copy in copies:
            copy.wait()
    else:
        slip_out[...] = fresh


def coarse_velocity_kernel(cv, cs, cm, xr, below, above, rows_ref, flags, out, xsend, next_rows, cs_near, cm_near):
    nx, ny, nz = cv.shape[1:]
    has_x, has_y = has(flags, BEFORE_X)[:, 0:128], has(flags, BEFORE_Z)[:, 0:128]
    more = has(flags, AFTER_Z)[:, 0:128]
    low, high = below.shape[0] - 24, above.shape[0] - 40
    cs_near[...] = cs[...]
    cm_near[...] = cm[...]
    xsend[...] = jnp.zeros_like(xsend)
    next_rows[3 * nx :, :] = jnp.zeros_like(next_rows[3 * nx :, :])

    def ahead(field, x):
        at = high + field * nx + x
        return jnp.where(more, above[at : at + 1, 0:128], 0.0)

    for x in range(nx):
        here = [cs[c, x] for c in COARSE_S]
        here_row = [ahead(3 + c, x) for c in COARSE_S]
        if x == 0:
            before, before_row = [], []
            for k in range(3):
                at = 96 + 8 * k
                plane = jnp.concatenate([xr[at : at + 8, 0:128], xr[at : at + 8, 128:256]], axis=0)
                before.append(jnp.where(has_x, plane, 0.0))
                before_row.append(jnp.where(has_x, xr[120 + k : 121 + k, 0:128], 0.0))
        else:
            before = [cs[c, x - 1] for c in (0, 3, 4)]
            before_row = [ahead(3 + c, x - 1) for c in (0, 3, 4)]
        rows = [jnp.where(has_y, below[low + k * nx + x : low + k * nx + x + 1, 0:128], 0.0) for k in range(3)]
        new = velocity_plane([cv[c, x] for c in COARSE_V], here, before, rows, cm[0, x])
        last = [here[k][ny - 1 : ny] for k in (3, 1, 5)]
        old_row = [ahead(c, x) for c in COARSE_V]
        new_row = velocity_plane(old_row, here_row, before_row, last, ahead(9, x), lambda a, edge: edge)
        for c in range(3):
            out[c, x] = new[c]
            next_rows[c * nx + x : c * nx + x + 1, :] = new_row[c]
            if x == 0:
                xsend[8 * c : 8 * c + 8, 0:128] = new[c][0:8]
                xsend[8 * c : 8 * c + 8, 128:256] = new[c][8:16]
    for f in range(2):
        xsend[24 + f : 25 + f, 0:128] = rows_ref[f, 0:1, :].astype(F32)


def coarse_stress_kernel(cv, cs, cm, xr, zr, rows_ref, rest, rest_next, flags, _, v_out, s_out):
    nx, ny, nz = cv.shape[1:]
    base = xr.shape[0] - 32
    has_x, has_y = has(flags, AFTER_X)[:, 0:128], has(flags, AFTER_Z)[:, 0:128]
    row_ids = own_rows(flags, (ny, nz))

    def inserted(plane, c, x):
        for f in range(2):
            if x < nx:
                hit = row_ids == rows_ref[f, x : x + 1, :].astype(F32)
            else:
                hit = row_ids == xr[base + 24 + f : base + 25 + f, 0:128]
            at = (f * 3 + c) * nx + x % nx
            value = rest[at : at + 1, :] if x < nx else rest_next[at : at + 1, :]
            plane = jnp.where(hit, value, plane)
        return plane

    planes = [[inserted(cv[c, x], c, x) for c in range(3)] for x in range(nx)]
    edge = []
    for c in range(3):
        at = base + 8 * c
        plane = jnp.concatenate([xr[at : at + 8, 0:128], xr[at : at + 8, 128:256]], axis=0)
        edge.append(jnp.where(has_x, inserted(plane, c, nx), 0.0))
    planes.append(edge)
    for x in range(nx):
        for c in range(3):
            v_out[c, x] = planes[x][c]
        rows = [jnp.where(has_y, zr[k * nx + x : k * nx + x + 1, :], 0.0) for k in range(3)]
        new = stress_plane([cs[c, x] for c in COARSE_S], planes[x], planes[x + 1], rows, cm[1, x], cm[2, x])
        for c in range(6):
            s_out[c, x] = new[c]


def swap(value, axis, bit):
    count = lax.axis_size(axis)
    return lax.ppermute(value, axis, [(i, i ^ bit) for i in range(count)])


def apart(value, out):
    parts = []
    for turn in range(1, 8):
        pairs = [(home, 2 * ((home // 2 + turn) % 8) + home % 2) for home in (5, 10)]
        parts.append(lax.ppermute(value, "gy", [pair if out else pair[::-1] for pair in pairs]))
    return parts


def body(
    coarse_velocity,
    coarse_stress,
    coarse_material,
    fine_velocity,
    fine_stress,
    fine_material,
    fault_slip,
    initial_shear,
    normal_stress,
    fault_mask,
    zone_ids,
    static_friction,
    friction_drop,
    weakening_distance,
    owner_rows,
):
    nx, nz, ny = fine_velocity.shape[1:]
    cx, cy, cz = coarse_velocity.shape[1:]
    flags = make_flags(nz // 3, cy)
    shares = (6 * cx, cz)
    fault = (fault_slip, initial_shear, normal_stress, fault_mask, zone_ids)
    fields = (fine_velocity, fine_stress, fine_material)
    zoned = (static_friction, friction_drop, weakening_distance)
    given = [
        pltpu.with_memory_space_constraint(a, pltpu.HBM)
        for a in fields + (coarse_stress, coarse_velocity, coarse_material) + fault + zoned + (owner_rows,)
    ]
    up, down, raw = pl.pallas_call(
        pack_kernel,
        out_shape=[
            jax.ShapeDtypeStruct(shape, F32) for shape in ((nx * 32 + 24, ny), (nx * 40 + 48, ny), (nz, 128))
        ],
        in_specs=[HBM] * 14 + [VMEM],
        out_specs=[VMEM] * 3,
        scratch_shapes=[pltpu.VMEM((a.shape[0], nx, 8, ny), F32) for a in fields * 2]
        + [pltpu.VMEM((c, cx, 8, cz), F32) for c in (3, 3, 6)]
        + [pltpu.VMEM((cx, 8, cz), F32)]
        + [pltpu.SMEM(a.shape, F32) for a in zoned]
        + [pltpu.VMEM(a.shape, a.dtype) for a in fault]
        + [pltpu.VMEM((128, 128), F32), pltpu.SemaphoreType.DMA((20,))],
        compiler_params=PARAMS,
    )(*given[:14], flags)
    coupling = pl.pallas_call(
        coupling_kernel,
        out_shape=jax.ShapeDtypeStruct(shares, F32),
        in_specs=[HBM] * 2 + [VMEM] * 2,
        out_specs=VMEM,
        scratch_shapes=[
            pltpu.VMEM(coarse_velocity.shape, F32),
            pltpu.VMEM(owner_rows.shape, jnp.int32),
            pltpu.SemaphoreType.DMA((2,)),
        ],
        compiler_params=PARAMS,
    )(given[4], given[14], flags, raw)
    from_below, from_above = ring(up, "gy", 1), ring(down, "gy", -1)
    parts = apart(coupling, True)
    rim, xsend, settings = call(
        rim_kernel,
        [(12, nx, RIM, ny), (208, ny), (7, 32, 128)],
        [VMEM] * 7,
        from_below, from_above, fine_stress, fine_material, coarse_stress, raw, flags,
    )
    slip = settings[0]
    xr = ring(xsend, "gx", 1)
    bounds = coupling + sum(parts[1:], parts[0])
    bounds = (bounds, swap(bounds, "gy", 1))
    coarse_moved, cxs, coarse_zr, coarse_stress, coarse_material = call(
        coarse_velocity_kernel,
        [coarse_velocity.shape, (32, ny), (16, cz), coarse_stress.shape, coarse_material.shape],
        [VMEM] * 8,
        coarse_velocity, coarse_stress, coarse_material, xr, from_below, from_above, owner_rows, flags,
    )
    velocity, stress = fine_velocity, fine_stress

    def velocity_half(step, behind, *to_send):
        args = (velocity, stress, fine_material, rim, behind, *bounds, flags)
        near = (velocity, edges, *args[2:]) if step == 1 else args
        sends = call(
            lambda *refs: velocity_edge_kernel(step, *refs),
            [(96, ny), (96, ny)] if step == 0 else [(128, ny), (96, ny)] if step == 1 else [(72, ny)],
            [VMEM] * (8 + len(to_send) * (step < 2)), *near, *(to_send if step < 2 else ()),
        )
        sends = list(sends)
        moved = [ring(send, "gx", way) for send, way in zip(sends, (-1, 1))]
        (new,) = call(fine_velocity_kernel, [(3, nx, 32, ny)], [VMEM] * 8, *args)
        return (new, moved, *to_send) if step == 2 else (new, moved)

    def stress_half(step, xr, *more):
        return call(
            lambda *refs: fine_stress_kernel(step, *refs),
            [(6, nx, 32, ny), (32, 128), (96, ny)][: 2 + step], [VMEM] * (8 + len(more)),
            stress, velocity, fine_material, rim, xr, settings, slip, flags, *more,
        )

    given_behind = xr
    velocity, (xr, v_behind) = velocity_half(0, given_behind)
    edges, behind, slip_behind = call(
        stress_edge_kernel, [(6, len(EDGES), 32, ny), (96, ny), (32, 128)], [VMEM] * 10,
        stress, velocity, fine_material, rim, xr, settings, slip, flags, v_behind, given_behind,
    )
    stress, slip = stress_half(0, xr)
    velocity, (coarse_xr, v_behind) = velocity_half(1, behind, cxs)
    stress, slip, behind = stress_half(1, coarse_xr, v_behind, given_behind, behind, slip_behind)
    (share,) = call(share_kernel, [shares], [VMEM] * 7, velocity, stress, fine_material, behind, *bounds, flags)
    share = share + swap(share, "gy", 1)
    velocity, (xr,), share = velocity_half(2, behind, share)
    share, velocity = lax.optimization_barrier((share, velocity))
    parts = apart(share, False)
    restricted = share + sum(parts[1:], parts[0])
    restricted_next = ring(restricted, "gx", -1)
    stress, velocity, slip, mark = pl.pallas_call(
        lambda *refs: fine_stress_kernel(2, *refs),
        out_shape=[jax.ShapeDtypeStruct(a.shape, F32) for a in (fine_stress, fine_velocity, fault_slip, raw[0:8])],
        in_specs=[VMEM] * 8,
        out_specs=[pl.BlockSpec(memory_space=pl.ANY)] * 3 + [VMEM],
        scratch_shapes=[
            pltpu.VMEM((6, nx, 32, ny), F32),
            pltpu.VMEM(fault_slip.shape, F32),
            pltpu.SemaphoreType.DMA((2 * nx + 3,)),
        ],
        compiler_params=PARAMS,
    )(stress, velocity, fine_material, rim, xr, settings, slip, flags)
    coarse_next, coarse_stress_next = call(
        coarse_stress_kernel,
        [coarse_velocity.shape, coarse_stress.shape],
        [VMEM] * 10,
        coarse_moved, coarse_stress, coarse_material, coarse_xr, coarse_zr, owner_rows, restricted, restricted_next,
        flags, mark,
    )
    return (coarse_next, coarse_stress_next, velocity, stress, slip)


def solution(mesh):
    grid = P(None, "gx", "gy", None)
    plane = P("gx", "gy")
    return jax.shard_map(
        body,
        mesh=mesh,
        in_specs=(grid,) * 6 + (plane,) * 5 + (P(),) * 3 + (P(None, "gx", None),),
        out_specs=(grid,) * 4 + (plane,),
        check_vma=False,
    )
```
